32 devices in a mesh: groups: 2 (over x), gx: 8 (over z, y), gy: 2 (over core).
Axes of the slice: x: 2, y: 2, z: 4, core: 2. Of those that a mesh axis runs over, the one named last changes fastest.
Arguments:
- field: bfloat16 [512, 256, 8, 128], P(('groups', 'gx'), 'gy'), parts along dimension 0, may hold values from -6 to 6
- cotangent: bfloat16 [512, 256, 8, 128], P(('groups', 'gx'), 'gy'), parts along dimension 0, may hold values from -6 to 6
- spectral_weight: bfloat16 [24, 192, 64, 128], P(None, ('gx', 'gy')), may hold values from -6 to 6
- mix_weight: bfloat16 [64, 64], replicated, may hold values from -0.75 to 0.75
Outputs:
- mixed: bfloat16 [512, 256, 8, 128], P(('groups', 'gx'), 'gy'), parts along dimension 0
- field_grad: bfloat16 [512, 256, 8, 128], P(('groups', 'gx'), 'gy'), parts along dimension 0
- spectral_grad: float32 [48, 192, 64, 128], P('groups', ('gx', 'gy')), parts along dimension 0
- mix_grad: float32 [128, 64], P('groups'), parts along dimension 0
The draws below stay inside these ranges and needn't reach their ends.
There are 2 independent parts, one for each index of `groups`. The reference program is written for one: setup_inputs(seed, part) draws one part's arguments, and reference() takes and returns one part's arrays. A program takes and returns all parts, laid end to end along the dimension named above; an argument that names none is the same for every part. Nothing has to cross between parts.
All inputs are finite; a program needn't handle non-finite values.
Results may differ from the reference program's by a relative error of at most 0.0079.
Values may be sent and summed in bfloat16 or wider, within the bound.
A program may use at most 384 MiB of HBM per device.

```python
import math
import jax
import jax.numpy as jnp

C = 64
MODES = 24
X = 256
Y = 256
P_SIZE = 8
PAIRS = 192


def shard_levels(key, dims, shards, least, largest):
    factor_of = 1.0
    for axis_at, parts in shards:
        draws = jax.random.uniform(jax.random.fold_in(jax.random.fold_in(key, 6), axis_at), (parts,), jnp.float32, least / len(shards), largest / len(shards))
        factor_of = factor_of * jnp.repeat(jnp.exp(draws), dims[axis_at] // parts).reshape((-1,) + (1,) * (len(dims) - 1 - axis_at))
    return factor_of


def bell_draw(own_key, shape, scale, most, split=(), kind=jnp.bfloat16):
    values = scale * jax.random.normal(own_key, shape, jnp.float32)
    if split:
        values = values * shard_levels(own_key, shape, split, -0.22, 0.18)
    return jnp.clip(values, -most, most).astype(kind)


def setup_inputs(seed: int = 0, part: int = 0) -> dict:
    key_of = jax.random.split(jax.random.key(seed), 5)
    part_keys = jax.random.split(jax.random.fold_in(key_of[4], part), 5)
    return {
        "field": bell_draw(part_keys[0], (X, Y, P_SIZE, 2 * C), 1.0, 6.0, ((0, 8), (1, 2))),
        "cotangent": bell_draw(part_keys[1], (X, Y, P_SIZE, 2 * C), 1.0, 6.0, ((0, 8), (1, 2))),
        "spectral_weight": bell_draw(key_of[2], (MODES, PAIRS, C, 2 * C), ((X * Y / (MODES * MODES * C)) ** 0.5), 6.0, ((1, 16),)),
        "mix_weight": bell_draw(key_of[3], (C, C), C ** -0.5, 0.75),
    }


def wave_tables(length, modes, offset, count):
    index = jnp.arange(modes, dtype=jnp.int32)
    freqs = jnp.where(index < modes // 2, index, index - modes)
    places = offset + jnp.arange(count, dtype=jnp.int32)
    phase = freqs[:, None] * places[None, :] % length
    angle = phase.astype(jnp.float32) * (2.0 * math.pi / length)
    factor = 1.0 / math.sqrt(length)
    return ((jnp.cos(angle) * factor).astype(jnp.bfloat16), (jnp.sin(angle) * factor).astype(jnp.bfloat16))

def fold_forward(first, second, half):
    real = first[..., :half] + second[..., half:]
    imag = first[..., half:] - second[..., :half]
    return jnp.concatenate([real, imag], axis=-1)

def fold_inverse(first, second, half):
    real = first[..., :half] - second[..., half:]
    imag = first[..., half:] + second[..., :half]
    return jnp.concatenate([real, imag], axis=-1)

def reference(field, cotangent, spectral_weight, mix_weight):
    cos_y, sin_y = wave_tables(Y, MODES, 0, Y)
    cos_x, sin_x = wave_tables(X, MODES, 0, X)
    cos_y32 = cos_y.astype(jnp.float32)
    sin_y32 = sin_y.astype(jnp.float32)
    cos_x32 = cos_x.astype(jnp.float32)
    sin_x32 = sin_x.astype(jnp.float32)

    def transform(data):
        data32 = data.astype(jnp.float32)
        first = jnp.einsum('ky,xyps->kpxs', cos_y32, data32)
        second = jnp.einsum('ky,xyps->kpxs', sin_y32, data32)
        rows = fold_forward(first, second, C).astype(jnp.bfloat16)
        rows32 = rows.reshape(MODES * P_SIZE, X, 2 * C).astype(jnp.float32)
        first = jnp.einsum('kx,gxs->gks', cos_x32, rows32)
        second = jnp.einsum('kx,gxs->gks', sin_x32, rows32)
        return fold_forward(first, second, C).astype(jnp.bfloat16)

    def untransform(modes):
        modes32 = modes.astype(jnp.float32)
        first = jnp.einsum('kx,gks->gxs', cos_x32, modes32)
        second = jnp.einsum('kx,gks->gxs', sin_x32, modes32)
        rows = fold_inverse(first, second, C).astype(jnp.bfloat16)
        rows32 = rows.reshape(MODES, P_SIZE, X, 2 * C).astype(jnp.float32)
        first = jnp.einsum('ky,kpxs->xyps', cos_y32, rows32)
        second = jnp.einsum('ky,kpxs->xyps', sin_y32, rows32)
        return fold_inverse(first, second, C)
    hat_field = transform(field).astype(jnp.float32)
    hat_cotangent = transform(cotangent).astype(jnp.float32)
    weight32 = spectral_weight.astype(jnp.float32)
    first = jnp.einsum('gkc,kgcs->gks', hat_field[..., :C], weight32)
    second = jnp.einsum('gkc,kgcs->gks', hat_field[..., C:], weight32)
    out_modes = fold_inverse(first, second, C).astype(jnp.bfloat16)
    swapped = jnp.concatenate([hat_cotangent[..., C:], -hat_cotangent[..., :C]], axis=-1)
    back_modes = jnp.concatenate([jnp.einsum('gks,kgcs->gkc', hat_cotangent, weight32), jnp.einsum('gks,kgcs->gkc', swapped, weight32)], axis=-1).astype(jnp.bfloat16)
    field_real, field_imag = (hat_field[..., :C], hat_field[..., C:])
    cot_real, cot_imag = (hat_cotangent[..., :C], hat_cotangent[..., C:])
    grad_real = jnp.einsum('gkc,gko->kgco', field_real, cot_real) + jnp.einsum('gkc,gko->kgco', field_imag, cot_imag)
    grad_imag = jnp.einsum('gkc,gko->kgco', field_real, cot_imag) - jnp.einsum('gkc,gko->kgco', field_imag, cot_real)
    spectral_grad = jnp.concatenate([grad_real, grad_imag], axis=-1)
    field5 = field.astype(jnp.float32).reshape(X, Y, P_SIZE, 2, C)
    cot5 = cotangent.astype(jnp.float32).reshape(X, Y, P_SIZE, 2, C)
    matrix = mix_weight.astype(jnp.float32)
    direct = jnp.einsum('xyprc,cd->xyprd', field5, matrix).reshape(X, Y, P_SIZE, 2 * C)
    mixed = (direct + untransform(out_modes)).astype(jnp.bfloat16)
    direct_back = jnp.einsum('xyprd,cd->xyprc', cot5, matrix).reshape(X, Y, P_SIZE, 2 * C)
    field_grad = (direct_back + untransform(back_modes)).astype(jnp.bfloat16)
    mix_grad = jnp.einsum('xyprc,xyprd->cd', field5, cot5) / math.sqrt(2 * X * Y * P_SIZE)
    return (mixed, field_grad, spectral_grad, mix_grad)
```

```python
import functools
import math

import jax
import jax.numpy as jnp
import ml_dtypes
import numpy as np
from jax import lax
from jax.experimental import pallas as pl
from jax.experimental.pallas import tpu as pltpu
from jax.sharding import PartitionSpec as P

VMEM_LIMIT = 48 * 1024 * 1024
SLOTS = 32


def wave_tables(length, freqs):
    places = np.arange(length, dtype=np.int64)
    phase = (freqs[:, None] * places[None, :]) % length
    angle = phase.astype(np.float32) * np.float32(2.0 * math.pi / length)
    factor = np.float32(1.0 / math.sqrt(length))
    cos = (np.cos(angle) * factor).astype(ml_dtypes.bfloat16).astype(np.float32)
    sin = (np.sin(angle) * factor).astype(ml_dtypes.bfloat16).astype(np.float32)
    return cos, sin


def split_blocks(table, parts):
    shaped = table.reshape(table.shape[:-1] + (parts, -1))
    return np.moveaxis(shaped, -2, 0)


def make_tables(total_x, total_y, modes, pairs, nx, ny):
    half = modes // 2
    eye = np.eye(pairs, dtype=np.float32)
    cos, sin = wave_tables(total_y, np.arange(half + 1))
    slots = np.zeros((SLOTS, total_y), np.float32)
    slots[: half + 1] = cos
    slots[half + 1 : 2 * half + 1] = sin[1:]
    slots = split_blocks(slots, ny)
    y_fwd = np.einsum("bkn,pr->bkpnr", slots, eye)
    y_fwd = y_fwd[:, : 2 * half + 2].reshape(ny, (2 * half + 2) * pairs, -1)
    y_inv = np.einsum("bkn,pr->bnpkr", slots, eye).reshape(ny, -1, SLOTS * pairs)
    index = np.arange(modes)
    freqs = np.where(index < half, index, index - modes)
    cos, sin = wave_tables(total_x, freqs)
    both = split_blocks(np.stack([cos, sin]), nx)
    x_fwd = np.einsum("btqn,pr->btpqnr", both, eye).reshape(nx, 2 * pairs * modes, -1)
    x_inv = np.einsum("btqn,pr->btnprq", both, eye).reshape(nx, -1, pairs * modes)
    return [t.astype(ml_dtypes.bfloat16) for t in (y_fwd, y_inv, x_fwd, x_inv)]


def times_i(value, half):
    lane = lax.broadcasted_iota(jnp.int32, value.shape, 1)
    parts = [
        pltpu.roll(value[:, a : a + 2 * half], half, 1)
        for a in range(0, value.shape[1], 2 * half)
    ]
    swapped = jnp.concatenate(parts, axis=1) if len(parts) > 1 else parts[0]
    return jnp.where(lane % (2 * half) < half, -swapped, swapped)


def forward_kernel(modes, f_ref, c_ref, ty_ref, tx_ref, p_ref, g_ref, rows, total):
    step = pl.program_id(0)
    block, _, doubled = f_ref.shape
    half, pairs = modes // 2, rows.shape[2]
    channels = doubled // 2

    @pl.when(step == 0)
    def _():
        total[...] = jnp.zeros_like(total)

    def one(i, carry):
        f, c = f_ref[i], c_ref[i]
        both = jnp.concatenate([f, c], axis=1)
        t = jnp.dot(ty_ref[...], both, preferred_element_type=jnp.float32)
        cut = (half + 1) * pairs
        cos = t[:cut]
        sin = times_i(t[cut : cut + half * pairs], channels)
        at = step * block + i
        rows[at, 0] = cos[:pairs]
        for m in range(1, half + 1):
            even = cos[m * pairs : (m + 1) * pairs]
            odd = sin[(m - 1) * pairs : m * pairs]
            if m < half:
                rows[at, m] = even - odd
            rows[at, modes - m] = even + odd
        total[...] += lax.dot_general(
            f, c, (((0,), (0,)), ((), ())), preferred_element_type=jnp.float32
        )
        return carry

    lax.fori_loop(0, block, one, 0)

    @pl.when(step == pl.num_programs(0) - 1)
    def _():
        def mode(k, carry):
            data = rows[:, k].reshape(-1, 2 * doubled).astype(jnp.bfloat16)
            t = jnp.dot(tx_ref[...], data, preferred_element_type=jnp.float32)
            n = pairs * modes
            hat = t[:n] - times_i(t[n:], channels)
            p_ref[pl.ds(k * pairs, pairs)] = hat.reshape(pairs, modes, 2 * doubled).astype(
                jnp.bfloat16
            )
            return carry

        lax.fori_loop(0, modes, mode, 0)
        g_ref[...] = total[:channels, :channels] + total[channels:, channels:]


def barrier_with(n, me, core):
    barrier = pltpu.get_barrier_semaphore()
    pl.semaphore_signal(barrier, inc=1, device_id={"gy": 1 - core})

    def greet(s, carry):
        pl.semaphore_signal(barrier, inc=1, device_id={"gx": lax.rem(me + s, n)})
        return carry

    lax.fori_loop(1, n, greet, 0)
    pl.semaphore_wait(barrier, n)


def reduce_kernel(
    n, scale, p_ref, g_ref, hat_ref, mix_ref, got, mine, parts, g_got, g_all,
    send1, recv1, send2, recv2, g_send, g_recv, g_send2, g_recv2,
):
    me, core = lax.axis_index("gx"), lax.axis_index("gy")
    barrier_with(n, me, core)

    def to_core(j):
        return pltpu.make_async_remote_copy(
            src_ref=p_ref.at[j, 1 - core], dst_ref=got.at[j],
            send_sem=send1.at[j], recv_sem=recv1.at[j], device_id={"gy": 1 - core},
        )

    def to_owner(j, slot):
        return pltpu.make_async_remote_copy(
            src_ref=mine.at[j], dst_ref=parts.at[slot],
            send_sem=send2.at[j], recv_sem=recv2.at[slot], device_id={"gx": j},
        )

    def g_to(j, slot):
        return pltpu.make_async_remote_copy(
            src_ref=g_all.at[me], dst_ref=g_all.at[slot],
            send_sem=g_send2.at[j], recv_sem=g_recv2.at[slot], device_id={"gx": j},
        )

    g_core = pltpu.make_async_remote_copy(
        src_ref=g_ref, dst_ref=g_got, send_sem=g_send, recv_sem=g_recv,
        device_id={"gy": 1 - core},
    )

    def start_core(s, carry):
        to_core(lax.rem(me + s, n)).start()
        return carry

    lax.fori_loop(1, n + 1, start_core, 0)
    g_core.start()

    def combine(s, carry):
        j = lax.rem(me + s, n)
        to_core(j).wait_recv()
        mine[j] = (
            p_ref[j, core].astype(jnp.float32) + got[j].astype(jnp.float32)
        ).astype(jnp.bfloat16)

        @pl.when(s < n)
        def _():
            to_owner(j, me).start()

        return carry

    lax.fori_loop(1, n + 1, combine, 0)
    g_core.wait_recv()
    g_all[me] = g_ref[...] + g_got[...]

    def start_g(s, carry):
        g_to(lax.rem(me + s, n), me).start()
        return carry

    lax.fori_loop(1, n, start_g, 0)
    hat_ref[...] = mine[me].astype(jnp.float32)

    def collect(s, carry):
        j = lax.rem(me + n - s, n)
        to_owner(j, j).wait_recv()
        hat_ref[...] += parts[j].astype(jnp.float32)
        g_to(j, j).wait_recv()
        return carry

    lax.fori_loop(1, n, collect, 0)
    mix = g_all[0]
    for j in range(1, n):
        mix = mix + g_all[j]
    mix_ref[...] = mix * scale

    def drain(s, carry):
        j = lax.rem(me + s, n)
        to_core(j).wait_send()

        @pl.when(s < n)
        def _():
            to_owner(j, me).wait_send()
            g_to(j, me).wait_send()

        return carry

    lax.fori_loop(1, n + 1, drain, 0)
    g_core.wait_send()


def gather_kernel(n, z_ref, all_ref, send1, recv1, send2, recv2):
    me, core = lax.axis_index("gx"), lax.axis_index("gy")
    barrier_with(n, me, core)
    all_ref[me, core] = z_ref[...]

    def to_peer(j, slot):
        return pltpu.make_async_remote_copy(
            src_ref=all_ref.at[me, core], dst_ref=all_ref.at[slot, core],
            send_sem=send1.at[j], recv_sem=recv1.at[slot], device_id={"gx": j},
        )

    def to_core(j, side):
        return pltpu.make_async_remote_copy(
            src_ref=all_ref.at[j, side], dst_ref=all_ref.at[j, side],
            send_sem=send2.at[j], recv_sem=recv2.at[j], device_id={"gy": 1 - core},
        )

    def start(s, carry):
        to_peer(lax.rem(me + s, n), me).start()
        return carry

    lax.fori_loop(1, n, start, 0)
    to_core(me, core).start()

    def forward(s, carry):
        j = lax.rem(me + n - s, n)
        to_peer(j, j).wait_recv()
        to_core(j, core).start()
        return carry

    lax.fori_loop(1, n, forward, 0)

    def finish(s, carry):
        j = lax.rem(me + n - s, n)
        to_core(j, 1 - core).wait_recv()
        to_core(j, core).wait_send()
        return carry

    lax.fori_loop(0, n, finish, 0)

    def drain(s, carry):
        to_peer(lax.rem(me + s, n), me).wait_send()
        return carry

    lax.fori_loop(1, n, drain, 0)


def modes_kernel(hat_ref, turned_ref, w_ref, z_ref, grad_ref):
    block, count, channels, doubled = w_ref.shape
    rows = lax.broadcasted_iota(jnp.int32, (8, doubled), 0)

    def one(i, carry):
        for g in range(count):
            cot = hat_ref[i, g : g + 1, doubled:]
            turned = -times_i(cot, channels)
            real = turned_ref[i, :channels, g : g + 1]
            imag = turned_ref[i, channels:doubled, g : g + 1]
            weight16 = w_ref[i, g]
            weight = weight16.astype(jnp.float32)
            grad_ref[i, g] = real * cot + imag * turned
            first = jnp.sum(real * weight, axis=0, keepdims=True)
            second = jnp.sum(imag * weight, axis=0, keepdims=True)
            z_ref[i, g : g + 1, :doubled] = first + times_i(second, channels)
            sides = jnp.where(rows == 0, cot, turned).astype(jnp.bfloat16)
            back = lax.dot_general(
                sides, weight16, (((1,), (1,)), ((), ())), preferred_element_type=jnp.float32
            )
            z_ref[i, g : g + 1, doubled:] = jnp.concatenate([back[0:1], back[1:2]], axis=1)
        return carry

    lax.fori_loop(0, block, one, 0)


def inverse_kernel(modes, f_ref, c_ref, z_ref, ty_ref, tx_ref, mix_ref, o_ref, b_ref, spread):
    step = pl.program_id(0)
    block, _, doubled = f_ref.shape
    half, pairs = modes // 2, spread.shape[2]
    channels = doubled // 2
    cells = spread.shape[0]

    @pl.when(step == 0)
    def _():
        def expand(k):
            data = z_ref[pl.ds(k * pairs, pairs)].reshape(pairs * modes, 2 * doubled)
            t = jnp.dot(
                tx_ref[...], data.astype(jnp.bfloat16), preferred_element_type=jnp.float32
            )
            n = cells * pairs
            return t[:n] + times_i(t[n:], channels)

        def put(slot, value):
            spread[:, slot] = value.reshape(cells, pairs, 2 * doubled)

        put(0, expand(0))

        def pair(m, carry):
            plus, minus = expand(m), expand(modes - m)
            put(m, plus + minus)
            put(half + m, times_i(plus - minus, channels))
            return carry

        lax.fori_loop(1, half, pair, 0)
        last = expand(half)
        put(half, last)
        put(2 * half, -times_i(last, channels))
        spread[:, 2 * half + 1 :] = jnp.zeros_like(spread[:, 2 * half + 1 :])

    def one(i, carry):
        modes_here = spread[step * block + i].reshape(-1, 2 * doubled).astype(jnp.bfloat16)
        left = jnp.concatenate([ty_ref[...], f_ref[i], c_ref[i]], axis=1)
        right = jnp.concatenate([modes_here, mix_ref[...]], axis=0)
        out = jnp.dot(left, right, preferred_element_type=jnp.float32)
        o_ref[i] = out[:, :doubled].astype(jnp.bfloat16)
        b_ref[i] = out[:, doubled:].astype(jnp.bfloat16)
        return carry

    lax.fori_loop(0, block, one, 0)


def whole(shape):
    zeros = (0,) * len(shape)
    return pl.BlockSpec(shape, lambda i: zeros)


def on_device(field, cotangent, spectral_weight, mix_weight):
    x_cells, y_cells, pairs, doubled = field.shape
    channels = doubled // 2
    modes = spectral_weight.shape[0]
    count = spectral_weight.shape[1]
    nx, ny = lax.axis_size("gx"), lax.axis_size("gy")
    total_x, total_y = x_cells * nx, y_cells * ny
    me, core = lax.axis_index("gx"), lax.axis_index("gy")
    tables = make_tables(total_x, total_y, modes, pairs, nx, ny)
    ty_fwd, ty_inv, tx_fwd, tx_inv = [
        lax.dynamic_index_in_dim(jnp.asarray(t), at, 0, keepdims=False)
        for t, at in zip(tables, (core, core, me, me))
    ]
    flat = (x_cells, y_cells * pairs, doubled)
    field2, cot2 = field.reshape(flat), cotangent.reshape(flat)
    block = 4
    grid = (x_cells // block,)
    data_spec = pl.BlockSpec((block,) + flat[1:], lambda i: (i, 0, 0))
    wide = 2 * doubled
    groups = modes * pairs
    params = pltpu.CompilerParams(vmem_limit_bytes=VMEM_LIMIT)

    partial, grad_part = pl.pallas_call(
        functools.partial(forward_kernel, modes),
        grid=grid,
        out_shape=(
            jax.ShapeDtypeStruct((groups, modes, wide), jnp.bfloat16),
            jax.ShapeDtypeStruct((channels, channels), jnp.float32),
        ),
        in_specs=[data_spec, data_spec, whole(ty_fwd.shape), whole(tx_fwd.shape)],
        out_specs=(whole((groups, modes, wide)), whole((channels, channels))),
        scratch_shapes=[
            pltpu.VMEM((x_cells, modes, pairs, wide), jnp.float32),
            pltpu.VMEM((doubled, doubled), jnp.float32),
        ],
        compiler_params=params,
        name="forward",
    )(field2, cot2, ty_fwd, tx_fwd)

    vmem = pl.BlockSpec(memory_space=pltpu.VMEM)
    share = (count, modes, wide)
    dma = pltpu.SemaphoreType.DMA
    hat, mix_grad = pl.pallas_call(
        functools.partial(
            reduce_kernel, nx, 1.0 / math.sqrt(2 * total_x * total_y * pairs)
        ),
        out_shape=(
            jax.ShapeDtypeStruct(share, jnp.float32),
            jax.ShapeDtypeStruct((channels, channels), jnp.float32),
        ),
        in_specs=[vmem, vmem],
        out_specs=(vmem, vmem),
        scratch_shapes=[
            pltpu.VMEM((nx,) + share, jnp.bfloat16),
            pltpu.VMEM((nx,) + share, jnp.bfloat16),
            pltpu.VMEM((nx,) + share, jnp.bfloat16),
            pltpu.VMEM((channels, channels), jnp.float32),
            pltpu.VMEM((nx, channels, channels), jnp.float32),
            dma((nx,)), dma((nx,)), dma((nx,)), dma((nx,)),
            dma, dma, dma((nx,)), dma((nx,)),
        ],
        compiler_params=pltpu.CompilerParams(
            collective_id=0, has_side_effects=True, vmem_limit_bytes=VMEM_LIMIT
        ),
        name="reduce",
    )(partial.reshape((nx, ny) + share), grad_part)

    hat = jnp.transpose(hat, (1, 0, 2)).astype(jnp.bfloat16).astype(jnp.float32)
    turned = jnp.transpose(hat[:, :, :doubled], (0, 2, 1))
    qb = 4
    z, spectral_grad = pl.pallas_call(
        modes_kernel,
        grid=(modes // qb,),
        out_shape=(
            jax.ShapeDtypeStruct((modes, count, wide), jnp.float32),
            jax.ShapeDtypeStruct((modes, count, channels, doubled), jnp.float32),
        ),
        in_specs=[
            pl.BlockSpec((qb, count, wide), lambda i: (i, 0, 0)),
            pl.BlockSpec((qb, doubled, count), lambda i: (i, 0, 0)),
            pl.BlockSpec((qb, count, channels, doubled), lambda i: (i, 0, 0, 0)),
        ],
        out_specs=(
            pl.BlockSpec((qb, count, wide), lambda i: (i, 0, 0)),
            pl.BlockSpec((qb, count, channels, doubled), lambda i: (i, 0, 0, 0)),
        ),
        compiler_params=params,
        name="modes",
    )(hat, turned, spectral_weight)
    z = jnp.transpose(z, (1, 0, 2)).astype(jnp.bfloat16)

    everything = pl.pallas_call(
        functools.partial(gather_kernel, nx),
        out_shape=jax.ShapeDtypeStruct((nx, ny) + share, jnp.bfloat16),
        in_specs=[vmem],
        out_specs=vmem,
        scratch_shapes=[dma((nx,)), dma((nx,)), dma((nx,)), dma((nx,))],
        compiler_params=pltpu.CompilerParams(
            collective_id=1, has_side_effects=True, vmem_limit_bytes=VMEM_LIMIT
        ),
        name="gather",
    )(z)

    empty = jnp.zeros_like(mix_weight)
    back = mix_weight.T
    rows = [
        [mix_weight if a == b else empty for b in range(2)] + [empty] * 2 for a in range(2)
    ] + [[empty] * 2 + [back if a == b else empty for b in range(2)] for a in range(2)]
    mixing = jnp.block(rows)
    mixed, field_grad = pl.pallas_call(
        functools.partial(inverse_kernel, modes),
        grid=grid,
        out_shape=(jax.ShapeDtypeStruct(flat, jnp.bfloat16),) * 2,
        in_specs=[
            data_spec, data_spec, whole((groups, modes, wide)),
            whole(ty_inv.shape), whole(tx_inv.shape), whole(mixing.shape),
        ],
        out_specs=(data_spec, data_spec),
        scratch_shapes=[pltpu.VMEM((x_cells, SLOTS, pairs, wide), jnp.float32)],
        compiler_params=params,
        name="inverse",
    )(field2, cot2, everything.reshape(groups, modes, wide), ty_inv, tx_inv, mixing)
    return (
        mixed.reshape(field.shape), field_grad.reshape(field.shape), spectral_grad, mix_grad
    )


def solution(mesh):
    placed = (
        P(("groups", "gx"), "gy", None, None),
        P(("groups", "gx"), "gy", None, None),
        P(None, ("gx", "gy"), None, None),
        P(),
    )
    return jax.shard_map(
        on_device,
        mesh=mesh,
        in_specs=placed,
        out_specs=(
            P(("groups", "gx"), "gy", None, None),
            P(("groups", "gx"), "gy", None, None),
            P("groups", ("gx", "gy"), None, None),
            P("groups", None),
        ),
        check_vma=False,
    )
```

```python
import functools
import math

import jax
import jax.numpy as jnp
import ml_dtypes
import numpy as np
from jax import lax
from jax.experimental import pallas as pl
from jax.experimental.pallas import tpu as pltpu
from jax.sharding import PartitionSpec as P

VMEM_LIMIT = 48 * 1024 * 1024
SLOTS = 32


def wave_tables(length, freqs):
    places = np.arange(length, dtype=np.int64)
    phase = (freqs[:, None] * places[None, :]) % length
    angle = phase.astype(np.float32) * np.float32(2.0 * math.pi / length)
    factor = np.float32(1.0 / math.sqrt(length))
    cos = (np.cos(angle) * factor).astype(ml_dtypes.bfloat16).astype(np.float32)
    sin = (np.sin(angle) * factor).astype(ml_dtypes.bfloat16).astype(np.float32)
    return cos, sin


def split_blocks(table, parts):
    shaped = table.reshape(table.shape[:-1] + (parts, -1))
    return np.moveaxis(shaped, -2, 0)


def make_tables(total_x, total_y, modes, pairs, nx, ny):
    half = modes // 2
    eye = np.eye(pairs, dtype=np.float32)
    cos, sin = wave_tables(total_y, np.arange(half + 1))
    slots = np.zeros((SLOTS, total_y), np.float32)
    slots[: half + 1] = cos
    slots[half + 1 : 2 * half + 1] = sin[1:]
    slots = split_blocks(slots, ny)
    y_fwd = np.einsum("bkn,pr->bkpnr", slots, eye)
    y_fwd = y_fwd[:, : 2 * half + 2].reshape(ny, (2 * half + 2) * pairs, -1)
    y_inv = np.einsum("bkn,pr->bnpkr", slots, eye).reshape(ny, -1, SLOTS * pairs)
    index = np.arange(modes)
    freqs = np.where(index < half, index, index - modes)
    cos, sin = wave_tables(total_x, freqs)
    both = split_blocks(np.stack([cos, sin]), nx)
    x_fwd = np.einsum("btqn,pr->btpqnr", both, eye).reshape(nx, 2 * pairs * modes, -1)
    x_inv = np.einsum("btqn,pr->btnprq", both, eye).reshape(nx, -1, pairs * modes)
    return [t.astype(ml_dtypes.bfloat16) for t in (y_fwd, y_inv, x_fwd, x_inv)]


def times_i(value, half):
    lane = lax.broadcasted_iota(jnp.int32, value.shape, 1)
    parts = [
        pltpu.roll(value[:, a : a + 2 * half], half, 1)
        for a in range(0, value.shape[1], 2 * half)
    ]
    swapped = jnp.concatenate(parts, axis=1) if len(parts) > 1 else parts[0]
    return jnp.where(lane % (2 * half) < half, -swapped, swapped)


def forward_kernel(modes, _, f_ref, c_ref, ty_ref, tx_ref, p_ref, rows):
    step = pl.program_id(0)
    block, _, doubled = f_ref.shape
    half, pairs = modes // 2, rows.shape[2]
    channels = doubled // 2

    def one(i, carry):
        f, c = f_ref[i], c_ref[i]
        both = jnp.concatenate([f, c], axis=1)
        t = jnp.dot(ty_ref[0], both, preferred_element_type=jnp.float32)
        cut = (half + 1) * pairs
        cos = t[:cut]
        sin = times_i(t[cut : cut + half * pairs], channels)
        at = step * block + i
        rows[at, 0] = cos[:pairs]
        for m in range(1, half + 1):
            even = cos[m * pairs : (m + 1) * pairs]
            odd = sin[(m - 1) * pairs : m * pairs]
            if m < half:
                rows[at, m] = even - odd
            rows[at, modes - m] = even + odd
        return carry

    lax.fori_loop(0, block, one, 0)

    @pl.when(step == pl.num_programs(0) - 1)
    def _():
        def mode(k, carry):
            data = rows[:, k].reshape(-1, 2 * doubled).astype(jnp.bfloat16)
            t = jnp.dot(tx_ref[0], data, preferred_element_type=jnp.float32)
            n = pairs * modes
            hat = t[:n] - times_i(t[n:], channels)
            p_ref[pl.ds(k * pairs, pairs)] = hat.reshape(pairs, modes, 2 * doubled).astype(
                jnp.bfloat16
            )
            return carry

        lax.fori_loop(0, modes, mode, 0)


def barrier_with(n, me, core):
    hosts = n // 2
    high, low = me // 2, lax.rem(me, 2)
    barrier = pltpu.get_barrier_semaphore()
    pl.semaphore_signal(barrier, inc=1, device_id={"gy": 1 - core})
    pl.semaphore_signal(barrier, inc=1, device_id={"gx": high * 2 + 1 - low})

    def greet(s, carry):
        h = lax.rem(high + s, hosts)
        pl.semaphore_signal(barrier, inc=1, device_id={"gx": h * 2 + low})
        return carry

    lax.fori_loop(1, hosts, greet, 0)
    pl.semaphore_wait(barrier, hosts + 1)


def reduce_kernel(
    n, p_ref, f_hbm, c_hbm, hat_ref, g_ref, got, mine, side, parts, f_buf, c_buf, total,
    send1, recv1, send2, recv2, send3, recv3, f_sem, c_sem,
):
    me, core = lax.axis_index("gx"), lax.axis_index("gy")
    hosts = n // 2
    high, low = me // 2, lax.rem(me, 2)
    block = f_buf.shape[1]
    chunks = f_hbm.shape[0] // block
    channels = total.shape[0] // 2

    def fetch(i, slot):
        return (
            pltpu.make_async_copy(
                f_hbm.at[pl.ds(i * block, block)], f_buf.at[slot], f_sem.at[slot]
            ),
            pltpu.make_async_copy(
                c_hbm.at[pl.ds(i * block, block)], c_buf.at[slot], c_sem.at[slot]
            ),
        )

    for i in range(min(2, chunks)):
        for copy in fetch(i, i):
            copy.start()
    total[...] = jnp.zeros_like(total)
    barrier_with(n, me, core)

    def to_core(j):
        return pltpu.make_async_remote_copy(
            src_ref=p_ref.at[j, 1 - core], dst_ref=got.at[j],
            send_sem=send1.at[j], recv_sem=recv1.at[j], device_id={"gy": 1 - core},
        )

    def to_partner(h):
        return pltpu.make_async_remote_copy(
            src_ref=mine.at[h, 1], dst_ref=side.at[h],
            send_sem=send2.at[h], recv_sem=recv2.at[h], device_id={"gx": high * 2 + 1 - low},
        )

    def to_owner(h, slot):
        return pltpu.make_async_remote_copy(
            src_ref=mine.at[h, 0], dst_ref=parts.at[slot],
            send_sem=send3.at[h], recv_sem=recv3.at[slot], device_id={"gx": h * 2 + low},
        )

    def add_products(first, last):
        def one(i, carry):
            slot = lax.rem(i, 2)
            for copy in fetch(i, slot):
                copy.wait()
            for b in range(block):
                total[...] += lax.dot_general(
                    f_buf[slot, b], c_buf[slot, b], (((0,), (0,)), ((), ())),
                    preferred_element_type=jnp.float32,
                )

            @pl.when(i + 2 < chunks)
            def _():
                for copy in fetch(i + 2, slot):
                    copy.start()

            return carry

        lax.fori_loop(first, last, one, 0)

    def start_core(s, carry):
        h = lax.rem(high + s, hosts)
        to_core(h * 2 + 1 - low).start()
        return carry

    def start_core_own(s, carry):
        h = lax.rem(high + s, hosts)
        to_core(h * 2 + low).start()
        return carry

    lax.fori_loop(1, hosts + 1, start_core, 0)
    lax.fori_loop(1, hosts + 1, start_core_own, 0)

    def pass_on(s, carry):
        h = lax.rem(high + s, hosts)
        j = h * 2 + 1 - low
        to_core(j).wait_recv()
        mine[h, 1] = (
            p_ref[j, core].astype(jnp.float32) + got[j].astype(jnp.float32)
        ).astype(jnp.bfloat16)
        to_partner(h).start()
        return carry

    lax.fori_loop(1, hosts + 1, pass_on, 0)
    add_products(0, chunks // 4)

    def combine(s, carry):
        h = lax.rem(high + s, hosts)
        j = h * 2 + low
        to_core(j).wait_recv()
        to_partner(h).wait_recv()
        hat_ref[...] = (
            p_ref[j, core].astype(jnp.float32)
            + got[j].astype(jnp.float32)
            + side[h].astype(jnp.float32)
        )

        @pl.when(s < hosts)
        def _():
            mine[h, 0] = hat_ref[...].astype(jnp.bfloat16)
            to_owner(h, high).start()

        return carry

    lax.fori_loop(1, hosts + 1, combine, 0)
    add_products(chunks // 4, chunks)
    g_ref[...] = total[:channels, :channels] + total[channels:, channels:]

    def collect(s, carry):
        h = lax.rem(high + hosts - s, hosts)
        to_owner(h, h).wait_recv()
        hat_ref[...] += parts[h].astype(jnp.float32)
        return carry

    lax.fori_loop(1, hosts, collect, 0)

    def drain(s, carry):
        h = lax.rem(high + s, hosts)
        to_core(h * 2).wait_send()
        to_core(h * 2 + 1).wait_send()
        to_partner(h).wait_send()

        @pl.when(s < hosts)
        def _():
            to_owner(h, high).wait_send()

        return carry

    lax.fori_loop(1, hosts + 1, drain, 0)


def gather_kernel(
    n, scale, z_ref, g_ref, all_ref, mix_ref, g_core, g_pair, g_side, g_all,
    send_up, send_down, recv_z, send_y, recv_y, send_c, recv_c,
    g_send, g_recv, g_send2, g_recv2, g_send3, g_recv3,
):
    me, core = lax.axis_index("gx"), lax.axis_index("gy")
    hosts = n // 2
    high, low = me // 2, lax.rem(me, 2)
    partner = high * 2 + 1 - low
    barrier_with(n, me, core)
    all_ref[me, core] = z_ref[...]

    def along(h, step, sems):
        block = all_ref.at[h * 2 + low, core]
        return pltpu.make_async_remote_copy(
            src_ref=block, dst_ref=block, send_sem=sems.at[h], recv_sem=recv_z.at[h],
            device_id={"gx": me + 2 * step},
        )

    def to_partner(h, side):
        block = all_ref.at[h * 2 + side, core]
        return pltpu.make_async_remote_copy(
            src_ref=block, dst_ref=block, send_sem=send_y.at[h], recv_sem=recv_y.at[h],
            device_id={"gx": partner},
        )

    def to_core(j, side):
        block = all_ref.at[j, side]
        return pltpu.make_async_remote_copy(
            src_ref=block, dst_ref=block, send_sem=send_c.at[j], recv_sem=recv_c.at[j],
            device_id={"gy": 1 - core},
        )

    def g_to_core():
        return pltpu.make_async_remote_copy(
            src_ref=g_ref, dst_ref=g_core, send_sem=g_send, recv_sem=g_recv,
            device_id={"gy": 1 - core},
        )

    def g_to_partner():
        return pltpu.make_async_remote_copy(
            src_ref=g_pair, dst_ref=g_side, send_sem=g_send2, recv_sem=g_recv2,
            device_id={"gx": partner},
        )

    def g_to(h, slot):
        return pltpu.make_async_remote_copy(
            src_ref=g_all.at[high], dst_ref=g_all.at[slot],
            send_sem=g_send3.at[h], recv_sem=g_recv3.at[slot], device_id={"gx": h * 2 + low},
        )

    has_up, has_down = high < hosts - 1, high > 0

    @pl.when(has_up)
    def _():
        along(high, 1, send_up).start()

    @pl.when(has_down)
    def _():
        along(high, -1, send_down).start()

    to_partner(high, low).start()
    to_core(me, core).start()
    g_to_core().start()

    def from_partner(h):
        to_partner(h, 1 - low).wait_recv()
        to_core(h * 2 + 1 - low, core).start()

    for t in range(1, hosts):
        below, above = high - t, high + t

        @pl.when(below >= 0)
        def _():
            along(below, 1, send_up).wait_recv()

            @pl.when(has_up)
            def _():
                along(below, 1, send_up).start()

            to_partner(below, low).start()
            to_core(below * 2 + low, core).start()

        @pl.when(above < hosts)
        def _():
            along(above, -1, send_down).wait_recv()

            @pl.when(has_down)
            def _():
                along(above, -1, send_down).start()

            to_partner(above, low).start()
            to_core(above * 2 + low, core).start()

        if t == 1:
            from_partner(high)
            g_to_core().wait_recv()
            g_pair[...] = g_ref[...] + g_core[...]
            g_to_partner().start()

    g_to_partner().wait_recv()
    g_all[high] = g_pair[...] + g_side[...]

    def start_g(s, carry):
        g_to(lax.rem(high + s, hosts), high).start()
        return carry

    lax.fori_loop(1, hosts, start_g, 0)

    for t in range(1, hosts):
        below, above = high - t, high + t

        @pl.when(below >= 0)
        def _():
            from_partner(below)

        @pl.when(above < hosts)
        def _():
            from_partner(above)

    def finish(s, carry):
        h = lax.rem(high + s, hosts)
        for side in range(2):
            to_core(h * 2 + side, 1 - core).wait_recv()
            to_core(h * 2 + side, core).wait_send()
        to_partner(h, low).wait_send()

        @pl.when(has_up & (h <= high))
        def _():
            along(h, 1, send_up).wait_send()

        @pl.when(has_down & (h >= high))
        def _():
            along(h, -1, send_down).wait_send()

        @pl.when(s > 0)
        def _():
            g_to(h, h).wait_recv()
            g_to(h, high).wait_send()

        return carry

    lax.fori_loop(0, hosts, finish, 0)
    g_to_core().wait_send()
    g_to_partner().wait_send()
    mix = g_all[0]
    for h in range(1, hosts):
        mix = mix + g_all[h]
    mix_ref[...] = mix * scale


def modes_kernel(hat_ref, turned_ref, w_ref, z_ref, grad_ref):
    block, count, channels, doubled = w_ref.shape
    rows = lax.broadcasted_iota(jnp.int32, (8, doubled), 0)

    def one(i, carry):
        for g in range(count):
            cot = hat_ref[i, g : g + 1, doubled:]
            turned = -times_i(cot, channels)
            real = turned_ref[i, :channels, g : g + 1]
            imag = turned_ref[i, channels:doubled, g : g + 1]
            weight16 = w_ref[i, g]
            weight = weight16.astype(jnp.float32)
            grad_ref[i, g] = real * cot + imag * turned
            first = jnp.sum(real * weight, axis=0, keepdims=True)
            second = jnp.sum(imag * weight, axis=0, keepdims=True)
            z_ref[i, g : g + 1, :doubled] = first + times_i(second, channels)
            sides = jnp.where(rows == 0, cot, turned).astype(jnp.bfloat16)
            back = lax.dot_general(
                sides, weight16, (((1,), (1,)), ((), ())), preferred_element_type=jnp.float32
            )
            z_ref[i, g : g + 1, doubled:] = jnp.concatenate([back[0:1], back[1:2]], axis=1)
        return carry

    lax.fori_loop(0, block, one, 0)


def inverse_kernel(modes, _, f_ref, c_ref, z_ref, ty_ref, tx_ref, mix_ref, o_ref, b_ref, spread):
    step = pl.program_id(0)
    block, _, doubled = f_ref.shape
    half, pairs = modes // 2, spread.shape[2]
    channels = doubled // 2
    cells = spread.shape[0]

    @pl.when(step == 0)
    def _():
        def expand(k):
            data = z_ref[pl.ds(k * pairs, pairs)].reshape(pairs * modes, 2 * doubled)
            t = jnp.dot(
                tx_ref[0], data.astype(jnp.bfloat16), preferred_element_type=jnp.float32
            )
            n = cells * pairs
            return t[:n] + times_i(t[n:], channels)

        def put(slot, value):
            spread[:, slot] = value.reshape(cells, pairs, 2 * doubled)

        put(0, expand(0))

        def pair(m, carry):
            plus, minus = expand(m), expand(modes - m)
            put(m, plus + minus)
            put(half + m, times_i(plus - minus, channels))
            return carry

        lax.fori_loop(1, half, pair, 0)
        last = expand(half)
        put(half, last)
        put(2 * half, -times_i(last, channels))
        spread[:, 2 * half + 1 :] = jnp.zeros_like(spread[:, 2 * half + 1 :])

    def one(i, carry):
        modes_here = spread[step * block + i].reshape(-1, 2 * doubled).astype(jnp.bfloat16)
        left = jnp.concatenate([ty_ref[0], f_ref[i], c_ref[i]], axis=1)
        right = jnp.concatenate([modes_here, mix_ref[...]], axis=0)
        out = jnp.dot(left, right, preferred_element_type=jnp.float32)
        o_ref[i] = out[:, :doubled].astype(jnp.bfloat16)
        b_ref[i] = out[:, doubled:].astype(jnp.bfloat16)
        return carry

    lax.fori_loop(0, block, one, 0)


def whole(shape):
    zeros = (0,) * len(shape)
    return pl.BlockSpec(shape, lambda i, where: zeros)


def one_of(table, axis):
    return pl.BlockSpec((1,) + table.shape[1:], lambda i, where: (where[axis], 0, 0))


def on_device(field, cotangent, spectral_weight, mix_weight):
    x_cells, y_cells, pairs, doubled = field.shape
    channels = doubled // 2
    modes = spectral_weight.shape[0]
    count = spectral_weight.shape[1]
    nx, ny = lax.axis_size("gx"), lax.axis_size("gy")
    total_x, total_y = x_cells * nx, y_cells * ny
    me, core = lax.axis_index("gx"), lax.axis_index("gy")
    tables = make_tables(total_x, total_y, modes, pairs, nx, ny)
    ty_fwd, ty_inv, tx_fwd, tx_inv = [jnp.asarray(t) for t in tables]
    where = jnp.stack([me, core]).astype(jnp.int32)
    flat = (x_cells, y_cells * pairs, doubled)
    field2, cot2 = field.reshape(flat), cotangent.reshape(flat)
    block = 4
    grid = (x_cells // block,)
    data_spec = pl.BlockSpec((block,) + flat[1:], lambda i, where: (i, 0, 0))
    wide = 2 * doubled
    groups = modes * pairs
    params = pltpu.CompilerParams(vmem_limit_bytes=VMEM_LIMIT)

    partial = pl.pallas_call(
        functools.partial(forward_kernel, modes),
        grid_spec=pltpu.PrefetchScalarGridSpec(
            num_scalar_prefetch=1,
            grid=grid,
            in_specs=[data_spec, data_spec, one_of(ty_fwd, 1), one_of(tx_fwd, 0)],
            out_specs=whole((groups, modes, wide)),
            scratch_shapes=[pltpu.VMEM((x_cells, modes, pairs, wide), jnp.float32)],
        ),
        out_shape=jax.ShapeDtypeStruct((groups, modes, wide), jnp.bfloat16),
        compiler_params=params,
        name="forward",
    )(where, field2, cot2, ty_fwd, tx_fwd)

    vmem = pl.BlockSpec(memory_space=pltpu.VMEM)
    hbm = pl.BlockSpec(memory_space=pl.ANY)
    share = (count, modes, wide)
    hosts = nx // 2
    dma = pltpu.SemaphoreType.DMA
    hat, grad_part = pl.pallas_call(
        functools.partial(reduce_kernel, nx),
        out_shape=(
            jax.ShapeDtypeStruct(share, jnp.float32),
            jax.ShapeDtypeStruct((channels, channels), jnp.float32),
        ),
        in_specs=[vmem, hbm, hbm],
        out_specs=(vmem, vmem),
        scratch_shapes=[
            pltpu.VMEM((nx,) + share, jnp.bfloat16),
            pltpu.VMEM((hosts, 2) + share, jnp.bfloat16),
            pltpu.VMEM((hosts,) + share, jnp.bfloat16),
            pltpu.VMEM((hosts,) + share, jnp.bfloat16),
            pltpu.VMEM((2, block) + flat[1:], jnp.bfloat16),
            pltpu.VMEM((2, block) + flat[1:], jnp.bfloat16),
            pltpu.VMEM((doubled, doubled), jnp.float32),
            dma((nx,)), dma((nx,)), dma((hosts,)), dma((hosts,)), dma((hosts,)), dma((hosts,)),
            dma((2,)), dma((2,)),
        ],
        compiler_params=pltpu.CompilerParams(
            collective_id=0, has_side_effects=True, vmem_limit_bytes=VMEM_LIMIT
        ),
        name="reduce",
    )(partial.reshape((nx, ny) + share), field2, cot2)

    hat = jnp.transpose(hat, (1, 0, 2)).astype(jnp.bfloat16).astype(jnp.float32)
    turned = jnp.transpose(hat[:, :, :doubled], (0, 2, 1))
    qb = 4
    z, spectral_grad = pl.pallas_call(
        modes_kernel,
        grid=(modes // qb,),
        out_shape=(
            jax.ShapeDtypeStruct((modes, count, wide), jnp.float32),
            jax.ShapeDtypeStruct((modes, count, channels, doubled), jnp.float32),
        ),
        in_specs=[
            pl.BlockSpec((qb, count, wide), lambda i: (i, 0, 0)),
            pl.BlockSpec((qb, doubled, count), lambda i: (i, 0, 0)),
            pl.BlockSpec((qb, count, channels, doubled), lambda i: (i, 0, 0, 0)),
        ],
        out_specs=(
            pl.BlockSpec((qb, count, wide), lambda i: (i, 0, 0)),
            pl.BlockSpec((qb, count, channels, doubled), lambda i: (i, 0, 0, 0)),
        ),
        compiler_params=params,
        name="modes",
    )(hat, turned, spectral_weight)
    z = jnp.transpose(z, (1, 0, 2)).astype(jnp.bfloat16)

    matrix = pltpu.VMEM((channels, channels), jnp.float32)
    everything, mix_grad = pl.pallas_call(
        functools.partial(
            gather_kernel, nx, 1.0 / math.sqrt(2 * total_x * total_y * pairs)
        ),
        out_shape=(
            jax.ShapeDtypeStruct((nx, ny) + share, jnp.bfloat16),
            jax.ShapeDtypeStruct((channels, channels), jnp.float32),
        ),
        in_specs=[vmem, vmem],
        out_specs=(vmem, vmem),
        scratch_shapes=[
            matrix, matrix, matrix, pltpu.VMEM((hosts, channels, channels), jnp.float32),
            dma((hosts,)), dma((hosts,)), dma((hosts,)), dma((hosts,)), dma((hosts,)),
            dma((nx,)), dma((nx,)), dma, dma, dma, dma, dma((hosts,)), dma((hosts,)),
        ],
        compiler_params=pltpu.CompilerParams(
            collective_id=1, has_side_effects=True, vmem_limit_bytes=VMEM_LIMIT
        ),
        name="gather",
    )(z, grad_part)

    empty = jnp.zeros_like(mix_weight)
    back = mix_weight.T
    rows = [
        [mix_weight if a == b else empty for b in range(2)] + [empty] * 2 for a in range(2)
    ] + [[empty] * 2 + [back if a == b else empty for b in range(2)] for a in range(2)]
    mixing = jnp.block(rows)
    mixed, field_grad = pl.pallas_call(
        functools.partial(inverse_kernel, modes),
        grid_spec=pltpu.PrefetchScalarGridSpec(
            num_scalar_prefetch=1,
            grid=grid,
            in_specs=[
                data_spec, data_spec, whole((groups, modes, wide)),
                one_of(ty_inv, 1), one_of(tx_inv, 0), whole(mixing.shape),
            ],
            out_specs=(data_spec, data_spec),
            scratch_shapes=[pltpu.VMEM((x_cells, SLOTS, pairs, wide), jnp.float32)],
        ),
        out_shape=(jax.ShapeDtypeStruct(flat, jnp.bfloat16),) * 2,
        compiler_params=params,
        name="inverse",
    )(where, field2, cot2, everything.reshape(groups, modes, wide), ty_inv, tx_inv, mixing)
    return (
        mixed.reshape(field.shape), field_grad.reshape(field.shape), spectral_grad, mix_grad
    )


def solution(mesh):
    placed = (
        P(("groups", "gx"), "gy", None, None),
        P(("groups", "gx"), "gy", None, None),
        P(None, ("gx", "gy"), None, None),
        P(),
    )
    return jax.shard_map(
        on_device,
        mesh=mesh,
        in_specs=placed,
        out_specs=(
            P(("groups", "gx"), "gy", None, None),
            P(("groups", "gx"), "gy", None, None),
            P("groups", ("gx", "gy"), None, None),
            P("groups", None),
        ),
        check_vma=False,
    )
```

```python
import functools
import math

import jax
import jax.numpy as jnp
import ml_dtypes
import numpy as np
from jax import lax
from jax.experimental import pallas as pl
from jax.experimental.pallas import tpu as pltpu
from jax.sharding import PartitionSpec as P

VMEM_LIMIT = 48 * 1024 * 1024
SLOTS = 32


def wave_tables(length, freqs):
    places = np.arange(length, dtype=np.int64)
    phase = (freqs[:, None] * places[None, :]) % length
    angle = phase.astype(np.float32) * np.float32(2.0 * math.pi / length)
    factor = np.float32(1.0 / math.sqrt(length))
    cos = (np.cos(angle) * factor).astype(ml_dtypes.bfloat16).astype(np.float32)
    sin = (np.sin(angle) * factor).astype(ml_dtypes.bfloat16).astype(np.float32)
    return cos, sin


def split_blocks(table, parts):
    shaped = table.reshape(table.shape[:-1] + (parts, -1))
    return np.moveaxis(shaped, -2, 0)


def make_tables(total_x, total_y, modes, pairs, nx, ny):
    half = modes // 2
    eye = np.eye(pairs, dtype=np.float32)
    cos, sin = wave_tables(total_y, np.arange(half + 1))
    slots = np.zeros((SLOTS, total_y), np.float32)
    slots[: half + 1] = cos
    slots[half + 1 : 2 * half + 1] = sin[1:]
    slots = split_blocks(slots, ny)
    y_fwd = np.einsum("bkn,pr->bkpnr", slots, eye)
    y_fwd = y_fwd[:, : 2 * half + 2].reshape(ny, (2 * half + 2) * pairs, -1)
    y_inv = np.einsum("bkn,pr->bnpkr", slots, eye).reshape(ny, -1, SLOTS * pairs)
    index = np.arange(modes)
    freqs = np.where(index < half, index, index - modes)
    cos, sin = wave_tables(total_x, freqs)
    both = split_blocks(np.stack([cos, sin]), nx)
    x_fwd = np.einsum("btqn,pr->btpqnr", both, eye).reshape(nx, 2 * pairs * modes, -1)
    x_inv = np.einsum("btqn,pr->btnprq", both, eye).reshape(nx, -1, pairs * modes)
    return [t.astype(ml_dtypes.bfloat16) for t in (y_fwd, y_inv, x_fwd, x_inv)]


def times_i(value, half):
    lane = lax.broadcasted_iota(jnp.int32, value.shape, 1)
    parts = [
        pltpu.roll(value[:, a : a + 2 * half], half, 1)
        for a in range(0, value.shape[1], 2 * half)
    ]
    swapped = jnp.concatenate(parts, axis=1) if len(parts) > 1 else parts[0]
    return jnp.where(lane % (2 * half) < half, -swapped, swapped)


def forward_kernel(modes, _, f_ref, c_ref, ty_ref, tx_ref, p_ref, rows):
    step = pl.program_id(0)
    block, _, doubled = f_ref.shape
    half, pairs = modes // 2, rows.shape[2]
    channels = doubled // 2

    def one(i, carry):
        f, c = f_ref[i], c_ref[i]
        both = jnp.concatenate([f, c], axis=1)
        t = jnp.dot(ty_ref[0], both, preferred_element_type=jnp.float32)
        cut = (half + 1) * pairs
        cos = t[:cut]
        sin = times_i(t[cut : cut + half * pairs], channels)
        at = step * block + i
        rows[at, 0] = cos[:pairs]
        for m in range(1, half + 1):
            even = cos[m * pairs : (m + 1) * pairs]
            odd = sin[(m - 1) * pairs : m * pairs]
            if m < half:
                rows[at, m] = even - odd
            rows[at, modes - m] = even + odd
        return carry

    lax.fori_loop(0, block, one, 0, unroll=4)

    @pl.when(step == pl.num_programs(0) - 1)
    def _():
        def mode(k, carry):
            data = rows[:, k].reshape(-1, 2 * doubled).astype(jnp.bfloat16)
            t = jnp.dot(tx_ref[0], data, preferred_element_type=jnp.float32)
            n = pairs * modes
            hat = t[:n] - times_i(t[n:], channels)
            p_ref[pl.ds(k * pairs, pairs)] = hat.reshape(pairs, modes, 2 * doubled).astype(
                jnp.bfloat16
            )
            return carry

        lax.fori_loop(0, modes, mode, 0, unroll=8)


def barrier_with(n, me, core):
    hosts = n // 2
    high, low = me // 2, lax.rem(me, 2)
    barrier = pltpu.get_barrier_semaphore()
    pl.semaphore_signal(barrier, inc=1, device_id={"gy": 1 - core})
    pl.semaphore_signal(barrier, inc=1, device_id={"gx": high * 2 + 1 - low})

    def greet(s, carry):
        h = lax.rem(high + s, hosts)
        pl.semaphore_signal(barrier, inc=1, device_id={"gx": h * 2 + low})
        return carry

    lax.fori_loop(1, hosts, greet, 0)
    pl.semaphore_wait(barrier, hosts + 1)


def reduce_kernel(
    n, p_ref, f_hbm, c_hbm, hat_ref, g_ref, got, mine, side, parts, f_buf, c_buf, total,
    send1, recv1, send2, recv2, send3, recv3, f_sem, c_sem,
):
    me, core = lax.axis_index("gx"), lax.axis_index("gy")
    hosts = n // 2
    high, low = me // 2, lax.rem(me, 2)
    block = f_buf.shape[1]
    chunks = f_hbm.shape[0] // block
    channels = total.shape[0] // 2

    def fetch(i, slot):
        return (
            pltpu.make_async_copy(
                f_hbm.at[pl.ds(i * block, block)], f_buf.at[slot], f_sem.at[slot]
            ),
            pltpu.make_async_copy(
                c_hbm.at[pl.ds(i * block, block)], c_buf.at[slot], c_sem.at[slot]
            ),
        )

    for i in range(min(2, chunks)):
        for copy in fetch(i, i):
            copy.start()
    total[...] = jnp.zeros_like(total)
    barrier_with(n, me, core)

    def to_core(j):
        return pltpu.make_async_remote_copy(
            src_ref=p_ref.at[j, 1 - core], dst_ref=got.at[j],
            send_sem=send1.at[j], recv_sem=recv1.at[j], device_id={"gy": 1 - core},
        )

    def to_partner(h):
        return pltpu.make_async_remote_copy(
            src_ref=mine.at[h, 1], dst_ref=side.at[h],
            send_sem=send2.at[h], recv_sem=recv2.at[h], device_id={"gx": high * 2 + 1 - low},
        )

    def to_owner(h, slot):
        return pltpu.make_async_remote_copy(
            src_ref=mine.at[h, 0], dst_ref=parts.at[slot],
            send_sem=send3.at[h], recv_sem=recv3.at[slot], device_id={"gx": h * 2 + low},
        )

    def add_products(first, last):
        def one(i, carry):
            slot = lax.rem(i, 2)
            for copy in fetch(i, slot):
                copy.wait()
            for b in range(block):
                total[...] += lax.dot_general(
                    f_buf[slot, b], c_buf[slot, b], (((0,), (0,)), ((), ())),
                    preferred_element_type=jnp.float32,
                )

            @pl.when(i + 2 < chunks)
            def _():
                for copy in fetch(i + 2, slot):
                    copy.start()

            return carry

        lax.fori_loop(first, last, one, 0)

    def start_core(s, carry):
        h = lax.rem(high + s, hosts)
        to_core(h * 2 + 1 - low).start()
        return carry

    def start_core_own(s, carry):
        h = lax.rem(high + s, hosts)
        to_core(h * 2 + low).start()
        return carry

    lax.fori_loop(1, hosts + 1, start_core, 0)
    lax.fori_loop(1, hosts + 1, start_core_own, 0)

    def pass_on(s, carry):
        h = lax.rem(high + s, hosts)
        j = h * 2 + 1 - low
        to_core(j).wait_recv()
        mine[h, 1] = (
            p_ref[j, core].astype(jnp.float32) + got[j].astype(jnp.float32)
        ).astype(jnp.bfloat16)
        to_partner(h).start()
        return carry

    lax.fori_loop(1, hosts + 1, pass_on, 0)
    add_products(0, chunks // 4)

    def combine(s, carry):
        h = lax.rem(high + s, hosts)
        j = h * 2 + low
        to_core(j).wait_recv()
        to_partner(h).wait_recv()
        hat_ref[...] = (
            p_ref[j, core].astype(jnp.float32)
            + got[j].astype(jnp.float32)
            + side[h].astype(jnp.float32)
        )

        @pl.when(s < hosts)
        def _():
            mine[h, 0] = hat_ref[...].astype(jnp.bfloat16)
            to_owner(h, high).start()

        return carry

    lax.fori_loop(1, hosts + 1, combine, 0)
    add_products(chunks // 4, chunks)
    g_ref[...] = total[:channels, :channels] + total[channels:, channels:]

    def collect(s, carry):
        h = lax.rem(high + hosts - s, hosts)
        to_owner(h, h).wait_recv()
        hat_ref[...] += parts[h].astype(jnp.float32)
        return carry

    lax.fori_loop(1, hosts, collect, 0)

    def drain(s, carry):
        h = lax.rem(high + s, hosts)
        to_core(h * 2).wait_send()
        to_core(h * 2 + 1).wait_send()
        to_partner(h).wait_send()

        @pl.when(s < hosts)
        def _():
            to_owner(h, high).wait_send()

        return carry

    lax.fori_loop(1, hosts + 1, drain, 0)


def gather_kernel(
    n, scale, z_ref, g_ref, all_ref, mix_ref, g_core, g_pair, g_side, g_all,
    send_up, send_down, recv_z, send_y, recv_y, send_c, recv_c,
    g_send, g_recv, g_send2, g_recv2, g_send3, g_recv3,
):
    me, core = lax.axis_index("gx"), lax.axis_index("gy")
    hosts = n // 2
    high, low = me // 2, lax.rem(me, 2)
    partner = high * 2 + 1 - low
    barrier_with(n, me, core)
    all_ref[me, core] = z_ref[...].astype(jnp.bfloat16)

    def along(h, step, sems):
        block = all_ref.at[h * 2 + low, core]
        return pltpu.make_async_remote_copy(
            src_ref=block, dst_ref=block, send_sem=sems.at[h], recv_sem=recv_z.at[h],
            device_id={"gx": me + 2 * step},
        )

    def to_partner(h, side):
        block = all_ref.at[h * 2 + side, core]
        return pltpu.make_async_remote_copy(
            src_ref=block, dst_ref=block, send_sem=send_y.at[h], recv_sem=recv_y.at[h],
            device_id={"gx": partner},
        )

    def to_core(j, side):
        block = all_ref.at[j, side]
        return pltpu.make_async_remote_copy(
            src_ref=block, dst_ref=block, send_sem=send_c.at[j], recv_sem=recv_c.at[j],
            device_id={"gy": 1 - core},
        )

    def g_to_core():
        return pltpu.make_async_remote_copy(
            src_ref=g_ref, dst_ref=g_core, send_sem=g_send, recv_sem=g_recv,
            device_id={"gy": 1 - core},
        )

    def g_to_partner():
        return pltpu.make_async_remote_copy(
            src_ref=g_pair, dst_ref=g_side, send_sem=g_send2, recv_sem=g_recv2,
            device_id={"gx": partner},
        )

    def g_to(h, slot):
        return pltpu.make_async_remote_copy(
            src_ref=g_all.at[high], dst_ref=g_all.at[slot],
            send_sem=g_send3.at[h], recv_sem=g_recv3.at[slot], device_id={"gx": h * 2 + low},
        )

    has_up, has_down = high < hosts - 1, high > 0

    @pl.when(has_up)
    def _():
        along(high, 1, send_up).start()

    @pl.when(has_down)
    def _():
        along(high, -1, send_down).start()

    to_partner(high, low).start()
    to_core(me, core).start()
    g_to_core().start()

    def from_partner(h):
        to_partner(h, 1 - low).wait_recv()
        to_core(h * 2 + 1 - low, core).start()

    for t in range(1, hosts):
        below, above = high - t, high + t

        @pl.when(below >= 0)
        def _():
            along(below, 1, send_up).wait_recv()

            @pl.when(has_up)
            def _():
                along(below, 1, send_up).start()

            to_partner(below, low).start()
            to_core(below * 2 + low, core).start()

        @pl.when(above < hosts)
        def _():
            along(above, -1, send_down).wait_recv()

            @pl.when(has_down)
            def _():
                along(above, -1, send_down).start()

            to_partner(above, low).start()
            to_core(above * 2 + low, core).start()

        if t == 1:
            from_partner(high)
            g_to_core().wait_recv()
            g_pair[...] = g_ref[...] + g_core[...]
            g_to_partner().start()

    g_to_partner().wait_recv()
    g_all[high] = g_pair[...] + g_side[...]

    def start_g(s, carry):
        g_to(lax.rem(high + s, hosts), high).start()
        return carry

    lax.fori_loop(1, hosts, start_g, 0)

    for t in range(1, hosts):
        below, above = high - t, high + t

        @pl.when(below >= 0)
        def _():
            from_partner(below)

        @pl.when(above < hosts)
        def _():
            from_partner(above)

    def finish(s, carry):
        h = lax.rem(high + s, hosts)
        for side in range(2):
            to_core(h * 2 + side, 1 - core).wait_recv()
            to_core(h * 2 + side, core).wait_send()
        to_partner(h, low).wait_send()

        @pl.when(has_up & (h <= high))
        def _():
            along(h, 1, send_up).wait_send()

        @pl.when(has_down & (h >= high))
        def _():
            along(h, -1, send_down).wait_send()

        @pl.when(s > 0)
        def _():
            g_to(h, h).wait_recv()
            g_to(h, high).wait_send()

        return carry

    lax.fori_loop(0, hosts, finish, 0)
    g_to_core().wait_send()
    g_to_partner().wait_send()
    mix = g_all[0]
    for h in range(1, hosts):
        mix = mix + g_all[h]
    mix_ref[...] = mix * scale


def modes_kernel(hat_ref, w_ref, z_ref, grad_ref):
    block, count, channels, doubled = w_ref.shape
    padded = -(-count // 8) * 8
    shape = (2 * padded, doubled)
    row = lax.broadcasted_iota(jnp.int32, shape, 0)
    lane = lax.broadcasted_iota(jnp.int32, shape, 1)
    pair = jnp.where(row >= padded, row - padded, row)
    right = (lane >= channels).astype(jnp.int32)
    left = lane[:padded] < channels
    tiles = -(-count // 2)

    for i in range(block):
        lines = [hat_ref[g, i : i + 1, :] for g in range(count)]
        if padded > count:
            lines.append(jnp.zeros((padded - count, 2 * doubled), jnp.float32))
        lines = jnp.concatenate(lines, axis=0)
        f, c = lines[:, :doubled], lines[:, doubled:]
        swapped = pltpu.roll(f, channels, 1)
        hat = jnp.concatenate(
            [jnp.where(left, f, swapped), jnp.where(left, swapped, f)], axis=0
        )
        cot = jnp.concatenate([c, -times_i(c, channels)], axis=0)
        weight = w_ref[i].reshape(count * channels, doubled)

        spaced = jnp.concatenate(
            [jnp.where(pair == 2 * t + right, hat, 0.0) for t in range(tiles)], axis=1
        )[:, : count * channels]
        both = jnp.dot(
            spaced.astype(jnp.bfloat16), weight, preferred_element_type=jnp.float32
        )
        out = both[:padded] + times_i(both[padded:], channels)

        every = lax.dot_general(
            cot.astype(jnp.bfloat16), weight, (((1,), (1,)), ((), ())),
            preferred_element_type=jnp.float32,
        )
        if count % 2:
            every = jnp.concatenate(
                [every, jnp.zeros((2 * padded, channels), jnp.float32)], axis=1
            )
        own = jnp.zeros(shape, jnp.float32)
        for t in range(tiles):
            tile = every[:, t * doubled : (t + 1) * doubled]
            own = own + jnp.where(pair == 2 * t + right, tile, 0.0)
        own = own + pltpu.roll(own, channels, 1)
        back = jnp.where(left, own[:padded], own[padded:])

        columns = jnp.transpose(hat)[:channels].astype(jnp.bfloat16)
        spread = jnp.concatenate(
            [jnp.where(pair == g, cot, 0.0) for g in range(count)], axis=1
        )
        grad = jnp.dot(
            columns, spread.astype(jnp.bfloat16), preferred_element_type=jnp.float32
        )
        for g in range(count):
            grad_ref[i, g] = grad[:, g * doubled : (g + 1) * doubled]
            z_ref[g, i : i + 1, :doubled] = out[g : g + 1]
            z_ref[g, i : i + 1, doubled:] = back[g : g + 1]


def inverse_kernel(modes, _, f_ref, c_ref, z_ref, ty_ref, tx_ref, mix_ref, o_ref, b_ref, spread):
    step = pl.program_id(0)
    block, _, doubled = f_ref.shape
    half, pairs = modes // 2, spread.shape[2]
    channels = doubled // 2
    cells = spread.shape[0]

    @pl.when(step == 0)
    def _():
        def expand(k):
            data = z_ref[pl.ds(k * pairs, pairs)].reshape(pairs * modes, 2 * doubled)
            t = jnp.dot(
                tx_ref[0], data.astype(jnp.bfloat16), preferred_element_type=jnp.float32
            )
            n = cells * pairs
            return t[:n] + times_i(t[n:], channels)

        def put(slot, value):
            spread[:, slot] = value.reshape(cells, pairs, 2 * doubled)

        put(0, expand(0))

        def pair(m, carry):
            plus, minus = expand(m), expand(modes - m)
            put(m, plus + minus)
            put(half + m, times_i(plus - minus, channels))
            return carry

        lax.fori_loop(1, half, pair, 0, unroll=6)
        last = expand(half)
        put(half, last)
        put(2 * half, -times_i(last, channels))
        spread[:, 2 * half + 1 :] = jnp.zeros_like(spread[:, 2 * half + 1 :])

    def one(i, carry):
        modes_here = spread[step * block + i].reshape(-1, 2 * doubled).astype(jnp.bfloat16)
        left = jnp.concatenate([ty_ref[0], f_ref[i], c_ref[i]], axis=1)
        right = jnp.concatenate([modes_here, mix_ref[...]], axis=0)
        out = jnp.dot(left, right, preferred_element_type=jnp.float32)
        o_ref[i] = out[:, :doubled].astype(jnp.bfloat16)
        b_ref[i] = out[:, doubled:].astype(jnp.bfloat16)
        return carry

    lax.fori_loop(0, block, one, 0, unroll=4)


def whole(shape):
    zeros = (0,) * len(shape)
    return pl.BlockSpec(shape, lambda i, where: zeros)


def one_of(table, axis):
    return pl.BlockSpec((1,) + table.shape[1:], lambda i, where: (where[axis], 0, 0))


def on_device(field, cotangent, spectral_weight, mix_weight):
    x_cells, y_cells, pairs, doubled = field.shape
    channels = doubled // 2
    modes = spectral_weight.shape[0]
    count = spectral_weight.shape[1]
    nx, ny = lax.axis_size("gx"), lax.axis_size("gy")
    total_x, total_y = x_cells * nx, y_cells * ny
    me, core = lax.axis_index("gx"), lax.axis_index("gy")
    tables = make_tables(total_x, total_y, modes, pairs, nx, ny)
    ty_fwd, ty_inv, tx_fwd, tx_inv = [jnp.asarray(t) for t in tables]
    where = jnp.stack([me, core]).astype(jnp.int32)
    flat = (x_cells, y_cells * pairs, doubled)
    field2, cot2 = field.reshape(flat), cotangent.reshape(flat)
    block = 4
    grid = (x_cells // block,)
    data_spec = pl.BlockSpec((block,) + flat[1:], lambda i, where: (i, 0, 0))
    wide = 2 * doubled
    groups = modes * pairs
    params = pltpu.CompilerParams(vmem_limit_bytes=VMEM_LIMIT)

    partial = pl.pallas_call(
        functools.partial(forward_kernel, modes),
        grid_spec=pltpu.PrefetchScalarGridSpec(
            num_scalar_prefetch=1,
            grid=grid,
            in_specs=[data_spec, data_spec, one_of(ty_fwd, 1), one_of(tx_fwd, 0)],
            out_specs=whole((groups, modes, wide)),
            scratch_shapes=[pltpu.VMEM((x_cells, modes, pairs, wide), jnp.float32)],
        ),
        out_shape=jax.ShapeDtypeStruct((groups, modes, wide), jnp.bfloat16),
        compiler_params=params,
        name="forward",
    )(where, field2, cot2, ty_fwd, tx_fwd)

    vmem = pl.BlockSpec(memory_space=pltpu.VMEM)
    hbm = pl.BlockSpec(memory_space=pl.ANY)
    share = (count, modes, wide)
    hosts = nx // 2
    dma = pltpu.SemaphoreType.DMA
    hat, grad_part = pl.pallas_call(
        functools.partial(reduce_kernel, nx),
        out_shape=(
            jax.ShapeDtypeStruct(share, jnp.float32),
            jax.ShapeDtypeStruct((channels, channels), jnp.float32),
        ),
        in_specs=[vmem, hbm, hbm],
        out_specs=(vmem, vmem),
        scratch_shapes=[
            pltpu.VMEM((nx,) + share, jnp.bfloat16),
            pltpu.VMEM((hosts, 2) + share, jnp.bfloat16),
            pltpu.VMEM((hosts,) + share, jnp.bfloat16),
            pltpu.VMEM((hosts,) + share, jnp.bfloat16),
            pltpu.VMEM((2, block) + flat[1:], jnp.bfloat16),
            pltpu.VMEM((2, block) + flat[1:], jnp.bfloat16),
            pltpu.VMEM((doubled, doubled), jnp.float32),
            dma((nx,)), dma((nx,)), dma((hosts,)), dma((hosts,)), dma((hosts,)), dma((hosts,)),
            dma((2,)), dma((2,)),
        ],
        compiler_params=pltpu.CompilerParams(
            collective_id=0, has_side_effects=True, vmem_limit_bytes=VMEM_LIMIT
        ),
        name="reduce",
    )(partial.reshape((nx, ny) + share), field2, cot2)

    qb = 8
    z, spectral_grad = pl.pallas_call(
        modes_kernel,
        grid=(modes // qb,),
        out_shape=(
            jax.ShapeDtypeStruct(share, jnp.float32),
            jax.ShapeDtypeStruct((modes, count, channels, doubled), jnp.float32),
        ),
        in_specs=[
            pl.BlockSpec((count, qb, wide), lambda i: (0, i, 0)),
            pl.BlockSpec((qb, count, channels, doubled), lambda i: (i, 0, 0, 0)),
        ],
        out_specs=(
            pl.BlockSpec((count, qb, wide), lambda i: (0, i, 0)),
            pl.BlockSpec((qb, count, channels, doubled), lambda i: (i, 0, 0, 0)),
        ),
        compiler_params=params,
        name="modes",
    )(hat, spectral_weight)

    matrix = pltpu.VMEM((channels, channels), jnp.float32)
    everything, mix_grad = pl.pallas_call(
        functools.partial(
            gather_kernel, nx, 1.0 / math.sqrt(2 * total_x * total_y * pairs)
        ),
        out_shape=(
            jax.ShapeDtypeStruct((nx, ny) + share, jnp.bfloat16),
            jax.ShapeDtypeStruct((channels, channels), jnp.float32),
        ),
        in_specs=[vmem, vmem],
        out_specs=(vmem, vmem),
        scratch_shapes=[
            matrix, matrix, matrix, pltpu.VMEM((hosts, channels, channels), jnp.float32),
            dma((hosts,)), dma((hosts,)), dma((hosts,)), dma((hosts,)), dma((hosts,)),
            dma((nx,)), dma((nx,)), dma, dma, dma, dma, dma((hosts,)), dma((hosts,)),
        ],
        compiler_params=pltpu.CompilerParams(
            collective_id=1, has_side_effects=True, vmem_limit_bytes=VMEM_LIMIT
        ),
        name="gather",
    )(z, grad_part)

    empty = jnp.zeros_like(mix_weight)
    back = mix_weight.T
    rows = [
        [mix_weight if a == b else empty for b in range(2)] + [empty] * 2 for a in range(2)
    ] + [[empty] * 2 + [back if a == b else empty for b in range(2)] for a in range(2)]
    mixing = jnp.block(rows)
    mixed, field_grad = pl.pallas_call(
        functools.partial(inverse_kernel, modes),
        grid_spec=pltpu.PrefetchScalarGridSpec(
            num_scalar_prefetch=1,
            grid=grid,
            in_specs=[
                data_spec, data_spec, whole((groups, modes, wide)),
                one_of(ty_inv, 1), one_of(tx_inv, 0), whole(mixing.shape),
            ],
            out_specs=(data_spec, data_spec),
            scratch_shapes=[pltpu.VMEM((x_cells, SLOTS, pairs, wide), jnp.float32)],
        ),
        out_shape=(jax.ShapeDtypeStruct(flat, jnp.bfloat16),) * 2,
        compiler_params=params,
        name="inverse",
    )(where, field2, cot2, everything.reshape(groups, modes, wide), ty_inv, tx_inv, mixing)
    return (
        mixed.reshape(field.shape), field_grad.reshape(field.shape), spectral_grad, mix_grad
    )


def solution(mesh):
    placed = (
        P(("groups", "gx"), "gy", None, None),
        P(("groups", "gx"), "gy", None, None),
        P(None, ("gx", "gy"), None, None),
        P(),
    )
    return jax.shard_map(
        on_device,
        mesh=mesh,
        in_specs=placed,
        out_specs=(
            P(("groups", "gx"), "gy", None, None),
            P(("groups", "gx"), "gy", None, None),
            P("groups", ("gx", "gy"), None, None),
            P("groups", None),
        ),
        check_vma=False,
    )
```

```python
import functools
import math

import jax
import jax.numpy as jnp
import ml_dtypes
import numpy as np
from jax import lax
from jax.experimental import pallas as pl
from jax.experimental.pallas import tpu as pltpu
from jax.sharding import PartitionSpec as P

VMEM_LIMIT = 48 * 1024 * 1024
SLOTS = 32


def wave_tables(length, freqs):
    places = np.arange(length, dtype=np.int64)
    phase = (freqs[:, None] * places[None, :]) % length
    angle = phase.astype(np.float32) * np.float32(2.0 * math.pi / length)
    factor = np.float32(1.0 / math.sqrt(length))
    cos = (np.cos(angle) * factor).astype(ml_dtypes.bfloat16).astype(np.float32)
    sin = (np.sin(angle) * factor).astype(ml_dtypes.bfloat16).astype(np.float32)
    return cos, sin


def split_blocks(table, parts):
    shaped = table.reshape(table.shape[:-1] + (parts, -1))
    return np.moveaxis(shaped, -2, 0)


def make_tables(total_x, total_y, modes, pairs, nx, ny):
    half = modes // 2
    eye = np.eye(pairs, dtype=np.float32)
    cos, sin = wave_tables(total_y, np.arange(half + 1))
    slots = np.zeros((SLOTS, total_y), np.float32)
    slots[: half + 1] = cos
    slots[half + 1 : 2 * half + 1] = sin[1:]
    slots = split_blocks(slots, ny)
    y_fwd = np.einsum("bkn,pr->bkpnr", slots, eye)
    y_fwd = y_fwd[:, : 2 * half + 2].reshape(ny, (2 * half + 2) * pairs, -1)
    y_inv = np.einsum("bkn,pr->bnpkr", slots, eye).reshape(ny, -1, SLOTS * pairs)
    index = np.arange(modes)
    freqs = np.where(index < half, index, index - modes)
    cos, sin = wave_tables(total_x, freqs)
    both = split_blocks(np.stack([cos, sin]), nx)
    x_fwd = np.einsum("btqn,pr->btpqnr", both, eye).reshape(nx, 2 * pairs * modes, -1)
    x_inv = np.einsum("btqn,pr->btnprq", both, eye).reshape(nx, -1, pairs * modes)
    return [t.astype(ml_dtypes.bfloat16) for t in (y_fwd, y_inv, x_fwd, x_inv)]


def times_i(value, half):
    lane = lax.broadcasted_iota(jnp.int32, value.shape, 1)
    parts = [
        pltpu.roll(value[:, a : a + 2 * half], half, 1)
        for a in range(0, value.shape[1], 2 * half)
    ]
    swapped = jnp.concatenate(parts, axis=1) if len(parts) > 1 else parts[0]
    return jnp.where(lane % (2 * half) < half, -swapped, swapped)


def forward_kernel(modes, _, f_ref, c_ref, ty_ref, tx_ref, p_ref, rows):
    step = pl.program_id(0)
    block, _, doubled = f_ref.shape
    half, pairs = modes // 2, rows.shape[2]
    channels = doubled // 2

    def one(i, carry):
        f, c = f_ref[i], c_ref[i]
        both = jnp.concatenate([f, c], axis=1)
        t = jnp.dot(ty_ref[0], both, preferred_element_type=jnp.float32)
        cut = (half + 1) * pairs
        cos = t[:cut]
        sin = times_i(t[cut : cut + half * pairs], channels)
        at = step * block + i
        rows[at, 0] = cos[:pairs]
        for m in range(1, half + 1):
            even = cos[m * pairs : (m + 1) * pairs]
            odd = sin[(m - 1) * pairs : m * pairs]
            if m < half:
                rows[at, m] = even - odd
            rows[at, modes - m] = even + odd
        return carry

    lax.fori_loop(0, block, one, 0, unroll=4)

    @pl.when(step == pl.num_programs(0) - 1)
    def _():
        def mode(k, carry):
            data = rows[:, k].reshape(-1, 2 * doubled).astype(jnp.bfloat16)
            t = jnp.dot(tx_ref[0], data, preferred_element_type=jnp.float32)
            n = pairs * modes
            hat = t[:n] - times_i(t[n:], channels)
            p_ref[pl.ds(k * pairs, pairs)] = hat.reshape(pairs, modes, 2 * doubled).astype(
                jnp.bfloat16
            )
            return carry

        lax.fori_loop(0, modes, mode, 0, unroll=modes)


def barrier_with(n, me, core):
    hosts = n // 2
    high, low = me // 2, lax.rem(me, 2)
    barrier = pltpu.get_barrier_semaphore()
    pl.semaphore_signal(barrier, inc=1, device_id={"gy": 1 - core})
    pl.semaphore_signal(barrier, inc=1, device_id={"gx": high * 2 + 1 - low})

    def greet(s, carry):
        h = lax.rem(high + s, hosts)
        pl.semaphore_signal(barrier, inc=1, device_id={"gx": h * 2 + low})
        return carry

    lax.fori_loop(1, hosts, greet, 0)
    pl.semaphore_wait(barrier, hosts + 1)


def reduce_kernel(
    n, p_ref, f_hbm, c_hbm, hat_ref, g_ref, got, mine, side, parts, f_buf, c_buf, total,
    send1, recv1, send2, recv2, send3, recv3, f_sem, c_sem,
):
    me, core = lax.axis_index("gx"), lax.axis_index("gy")
    hosts = n // 2
    high, low = me // 2, lax.rem(me, 2)
    block = f_buf.shape[1]
    chunks = f_hbm.shape[0] // block
    channels = total.shape[0] // 2

    def fetch(i, slot):
        return (
            pltpu.make_async_copy(
                f_hbm.at[pl.ds(i * block, block)], f_buf.at[slot], f_sem.at[slot]
            ),
            pltpu.make_async_copy(
                c_hbm.at[pl.ds(i * block, block)], c_buf.at[slot], c_sem.at[slot]
            ),
        )

    for i in range(min(2, chunks)):
        for copy in fetch(i, i):
            copy.start()
    total[...] = jnp.zeros_like(total)
    barrier_with(n, me, core)

    def to_core(j):
        return pltpu.make_async_remote_copy(
            src_ref=p_ref.at[j, 1 - core], dst_ref=got.at[j],
            send_sem=send1.at[j], recv_sem=recv1.at[j], device_id={"gy": 1 - core},
        )

    def to_partner(h):
        return pltpu.make_async_remote_copy(
            src_ref=mine.at[h, 1], dst_ref=side.at[h],
            send_sem=send2.at[h], recv_sem=recv2.at[h], device_id={"gx": high * 2 + 1 - low},
        )

    def to_owner(h, slot):
        return pltpu.make_async_remote_copy(
            src_ref=mine.at[h, 0], dst_ref=parts.at[slot],
            send_sem=send3.at[h], recv_sem=recv3.at[slot], device_id={"gx": h * 2 + low},
        )

    def add_products(first, last):
        def one(i, carry):
            slot = lax.rem(i, 2)
            for copy in fetch(i, slot):
                copy.wait()
            for b in range(block):
                total[...] += lax.dot_general(
                    f_buf[slot, b], c_buf[slot, b], (((0,), (0,)), ((), ())),
                    preferred_element_type=jnp.float32,
                )

            @pl.when(i + 2 < chunks)
            def _():
                for copy in fetch(i + 2, slot):
                    copy.start()

            return carry

        lax.fori_loop(first, last, one, 0)

    def start_core(s, carry):
        h = lax.rem(high + s, hosts)
        to_core(h * 2 + 1 - low).start()
        return carry

    def start_core_own(s, carry):
        h = lax.rem(high + s, hosts)
        to_core(h * 2 + low).start()
        return carry

    lax.fori_loop(1, hosts + 1, start_core, 0)
    lax.fori_loop(1, hosts + 1, start_core_own, 0)

    def pass_on(s, carry):
        h = lax.rem(high + s, hosts)
        j = h * 2 + 1 - low
        to_core(j).wait_recv()
        mine[h, 1] = (
            p_ref[j, core].astype(jnp.float32) + got[j].astype(jnp.float32)
        ).astype(jnp.bfloat16)
        to_partner(h).start()
        return carry

    lax.fori_loop(1, hosts + 1, pass_on, 0)
    add_products(0, chunks // 4)

    def combine(s, carry):
        h = lax.rem(high + s, hosts)
        j = h * 2 + low
        to_core(j).wait_recv()
        to_partner(h).wait_recv()
        hat_ref[...] = (
            p_ref[j, core].astype(jnp.float32)
            + got[j].astype(jnp.float32)
            + side[h].astype(jnp.float32)
        )

        @pl.when(s < hosts)
        def _():
            mine[h, 0] = hat_ref[...].astype(jnp.bfloat16)
            to_owner(h, high).start()

        return carry

    lax.fori_loop(1, hosts + 1, combine, 0)
    add_products(chunks // 4, chunks)
    g_ref[...] = total[:channels, :channels] + total[channels:, channels:]

    def collect(s, carry):
        h = lax.rem(high + hosts - s, hosts)
        to_owner(h, h).wait_recv()
        hat_ref[...] += parts[h].astype(jnp.float32)
        return carry

    lax.fori_loop(1, hosts, collect, 0)

    def drain(s, carry):
        h = lax.rem(high + s, hosts)
        to_core(h * 2).wait_send()
        to_core(h * 2 + 1).wait_send()
        to_partner(h).wait_send()

        @pl.when(s < hosts)
        def _():
            to_owner(h, high).wait_send()

        return carry

    lax.fori_loop(1, hosts + 1, drain, 0)


def gather_kernel(
    n, scale, z_ref, g_ref, all_ref, mix_ref, g_core, g_pair, g_side, g_all,
    send_up, send_down, recv_z, send_y, recv_y, send_c, recv_c,
    g_send, g_recv, g_send2, g_recv2, g_send3, g_recv3,
):
    me, core = lax.axis_index("gx"), lax.axis_index("gy")
    hosts = n // 2
    high, low = me // 2, lax.rem(me, 2)
    partner = high * 2 + 1 - low
    barrier_with(n, me, core)
    all_ref[me, core] = z_ref[...].astype(jnp.bfloat16)

    def along(h, step, sems):
        block = all_ref.at[h * 2 + low, core]
        return pltpu.make_async_remote_copy(
            src_ref=block, dst_ref=block, send_sem=sems.at[h], recv_sem=recv_z.at[h],
            device_id={"gx": me + 2 * step},
        )

    def to_partner(h, side):
        block = all_ref.at[h * 2 + side, core]
        return pltpu.make_async_remote_copy(
            src_ref=block, dst_ref=block, send_sem=send_y.at[h], recv_sem=recv_y.at[h],
            device_id={"gx": partner},
        )

    def to_core(j, side):
        block = all_ref.at[j, side]
        return pltpu.make_async_remote_copy(
            src_ref=block, dst_ref=block, send_sem=send_c.at[j], recv_sem=recv_c.at[j],
            device_id={"gy": 1 - core},
        )

    def g_to_core():
        return pltpu.make_async_remote_copy(
            src_ref=g_ref, dst_ref=g_core, send_sem=g_send, recv_sem=g_recv,
            device_id={"gy": 1 - core},
        )

    def g_to_partner():
        return pltpu.make_async_remote_copy(
            src_ref=g_pair, dst_ref=g_side, send_sem=g_send2, recv_sem=g_recv2,
            device_id={"gx": partner},
        )

    def g_to(h, slot):
        return pltpu.make_async_remote_copy(
            src_ref=g_all.at[high], dst_ref=g_all.at[slot],
            send_sem=g_send3.at[h], recv_sem=g_recv3.at[slot], device_id={"gx": h * 2 + low},
        )

    has_up, has_down = high < hosts - 1, high > 0

    @pl.when(has_up)
    def _():
        along(high, 1, send_up).start()

    @pl.when(has_down)
    def _():
        along(high, -1, send_down).start()

    to_partner(high, low).start()
    to_core(me, core).start()
    g_to_core().start()

    def from_partner(h):
        to_partner(h, 1 - low).wait_recv()
        to_core(h * 2 + 1 - low, core).start()

    for t in range(1, hosts):
        below, above = high - t, high + t

        @pl.when(below >= 0)
        def _():
            along(below, 1, send_up).wait_recv()

            @pl.when(has_up)
            def _():
                along(below, 1, send_up).start()

            to_partner(below, low).start()
            to_core(below * 2 + low, core).start()

        @pl.when(above < hosts)
        def _():
            along(above, -1, send_down).wait_recv()

            @pl.when(has_down)
            def _():
                along(above, -1, send_down).start()

            to_partner(above, low).start()
            to_core(above * 2 + low, core).start()

        if t == 1:
            from_partner(high)
            g_to_core().wait_recv()
            g_pair[...] = g_ref[...] + g_core[...]
            g_to_partner().start()

    g_to_partner().wait_recv()
    g_all[high] = g_pair[...] + g_side[...]

    def start_g(s, carry):
        g_to(lax.rem(high + s, hosts), high).start()
        return carry

    lax.fori_loop(1, hosts, start_g, 0)

    for t in range(1, hosts):
        below, above = high - t, high + t

        @pl.when(below >= 0)
        def _():
            from_partner(below)

        @pl.when(above < hosts)
        def _():
            from_partner(above)

    def finish(s, carry):
        h = lax.rem(high + s, hosts)
        for side in range(2):
            to_core(h * 2 + side, 1 - core).wait_recv()
            to_core(h * 2 + side, core).wait_send()
        to_partner(h, low).wait_send()

        @pl.when(has_up & (h <= high))
        def _():
            along(h, 1, send_up).wait_send()

        @pl.when(has_down & (h >= high))
        def _():
            along(h, -1, send_down).wait_send()

        @pl.when(s > 0)
        def _():
            g_to(h, h).wait_recv()
            g_to(h, high).wait_send()

        return carry

    lax.fori_loop(0, hosts, finish, 0)
    g_to_core().wait_send()
    g_to_partner().wait_send()
    mix = g_all[0]
    for h in range(1, hosts):
        mix = mix + g_all[h]
    mix_ref[...] = mix * scale


def modes_kernel(hat_ref, w_ref, z_ref, grad_ref):
    block, count, channels, doubled = w_ref.shape
    padded = -(-count // 8) * 8
    shape = (2 * padded, doubled)
    row = lax.broadcasted_iota(jnp.int32, shape, 0)
    lane = lax.broadcasted_iota(jnp.int32, shape, 1)
    pair = jnp.where(row >= padded, row - padded, row)
    right = (lane >= channels).astype(jnp.int32)
    left = lane[:padded] < channels
    tiles = -(-count // 2)

    for i in range(block):
        lines = [hat_ref[g, i : i + 1, :] for g in range(count)]
        if padded > count:
            lines.append(jnp.zeros((padded - count, 2 * doubled), jnp.float32))
        lines = jnp.concatenate(lines, axis=0)
        f, c = lines[:, :doubled], lines[:, doubled:]
        swapped = pltpu.roll(f, channels, 1)
        hat = jnp.concatenate(
            [jnp.where(left, f, swapped), jnp.where(left, swapped, f)], axis=0
        )
        cot = jnp.concatenate([c, -times_i(c, channels)], axis=0)
        weight = w_ref[i].reshape(count * channels, doubled)

        spaced = jnp.concatenate(
            [jnp.where(pair == 2 * t + right, hat, 0.0) for t in range(tiles)], axis=1
        )[:, : count * channels]
        both = jnp.dot(
            spaced.astype(jnp.bfloat16), weight, preferred_element_type=jnp.float32
        )
        out = both[:padded] + times_i(both[padded:], channels)

        every = lax.dot_general(
            cot.astype(jnp.bfloat16), weight, (((1,), (1,)), ((), ())),
            preferred_element_type=jnp.float32,
        )
        if count % 2:
            every = jnp.concatenate(
                [every, jnp.zeros((2 * padded, channels), jnp.float32)], axis=1
            )
        own = jnp.zeros(shape, jnp.float32)
        for t in range(tiles):
            tile = every[:, t * doubled : (t + 1) * doubled]
            own = own + jnp.where(pair == 2 * t + right, tile, 0.0)
        own = own + pltpu.roll(own, channels, 1)
        back = jnp.where(left, own[:padded], own[padded:])

        columns = jnp.transpose(hat)[:channels].astype(jnp.bfloat16)
        spread = jnp.concatenate(
            [jnp.where(pair == g, cot, 0.0) for g in range(count)], axis=1
        )
        grad = jnp.dot(
            columns, spread.astype(jnp.bfloat16), preferred_element_type=jnp.float32
        )
        for g in range(count):
            grad_ref[i, g] = grad[:, g * doubled : (g + 1) * doubled]
            z_ref[g, i : i + 1, :doubled] = out[g : g + 1]
            z_ref[g, i : i + 1, doubled:] = back[g : g + 1]


def inverse_kernel(modes, _, f_ref, c_ref, z_ref, ty_ref, tx_ref, mix_ref, o_ref, b_ref, spread):
    step = pl.program_id(0)
    block, _, doubled = f_ref.shape
    half, pairs = modes // 2, spread.shape[2]
    channels = doubled // 2
    cells = spread.shape[0]

    @pl.when(step == 0)
    def _():
        def expand(k):
            data = z_ref[pl.ds(k * pairs, pairs)].reshape(pairs * modes, 2 * doubled)
            t = jnp.dot(
                tx_ref[0], data.astype(jnp.bfloat16), preferred_element_type=jnp.float32
            )
            n = cells * pairs
            return t[:n] + times_i(t[n:], channels)

        def put(slot, value):
            spread[:, slot] = value.reshape(cells, pairs, 2 * doubled)

        put(0, expand(0))

        def pair(m, carry):
            plus, minus = expand(m), expand(modes - m)
            put(m, plus + minus)
            put(half + m, times_i(plus - minus, channels))
            return carry

        lax.fori_loop(1, half, pair, 0, unroll=half - 1)
        last = expand(half)
        put(half, last)
        put(2 * half, -times_i(last, channels))
        spread[:, 2 * half + 1 :] = jnp.zeros_like(spread[:, 2 * half + 1 :])

    def one(i, carry):
        modes_here = spread[step * block + i].reshape(-1, 2 * doubled).astype(jnp.bfloat16)
        left = jnp.concatenate([ty_ref[0], f_ref[i], c_ref[i]], axis=1)
        right = jnp.concatenate([modes_here, mix_ref[...]], axis=0)
        out = jnp.dot(left, right, preferred_element_type=jnp.float32)
        o_ref[i] = out[:, :doubled].astype(jnp.bfloat16)
        b_ref[i] = out[:, doubled:].astype(jnp.bfloat16)
        return carry

    lax.fori_loop(0, block, one, 0, unroll=4)


def whole(shape):
    zeros = (0,) * len(shape)
    return pl.BlockSpec(shape, lambda i, where: zeros)


def one_of(table, axis):
    return pl.BlockSpec((1,) + table.shape[1:], lambda i, where: (where[axis], 0, 0))


def on_device(field, cotangent, spectral_weight, mix_weight):
    x_cells, y_cells, pairs, doubled = field.shape
    channels = doubled // 2
    modes = spectral_weight.shape[0]
    count = spectral_weight.shape[1]
    nx, ny = lax.axis_size("gx"), lax.axis_size("gy")
    total_x, total_y = x_cells * nx, y_cells * ny
    me, core = lax.axis_index("gx"), lax.axis_index("gy")
    tables = make_tables(total_x, total_y, modes, pairs, nx, ny)
    ty_fwd, ty_inv, tx_fwd, tx_inv = [jnp.asarray(t) for t in tables]
    where = jnp.stack([me, core]).astype(jnp.int32)
    flat = (x_cells, y_cells * pairs, doubled)
    field2, cot2 = field.reshape(flat), cotangent.reshape(flat)
    block = 4
    grid = (x_cells // block,)
    data_spec = pl.BlockSpec((block,) + flat[1:], lambda i, where: (i, 0, 0))
    wide = 2 * doubled
    groups = modes * pairs
    params = pltpu.CompilerParams(vmem_limit_bytes=VMEM_LIMIT)

    partial = pl.pallas_call(
        functools.partial(forward_kernel, modes),
        grid_spec=pltpu.PrefetchScalarGridSpec(
            num_scalar_prefetch=1,
            grid=grid,
            in_specs=[data_spec, data_spec, one_of(ty_fwd, 1), one_of(tx_fwd, 0)],
            out_specs=whole((groups, modes, wide)),
            scratch_shapes=[pltpu.VMEM((x_cells, modes, pairs, wide), jnp.float32)],
        ),
        out_shape=jax.ShapeDtypeStruct((groups, modes, wide), jnp.bfloat16),
        compiler_params=params,
        name="forward",
    )(where, field2, cot2, ty_fwd, tx_fwd)

    vmem = pl.BlockSpec(memory_space=pltpu.VMEM)
    hbm = pl.BlockSpec(memory_space=pl.ANY)
    share = (count, modes, wide)
    hosts = nx // 2
    dma = pltpu.SemaphoreType.DMA
    hat, grad_part = pl.pallas_call(
        functools.partial(reduce_kernel, nx),
        out_shape=(
            jax.ShapeDtypeStruct(share, jnp.float32),
            jax.ShapeDtypeStruct((channels, channels), jnp.float32),
        ),
        in_specs=[vmem, hbm, hbm],
        out_specs=(vmem, vmem),
        scratch_shapes=[
            pltpu.VMEM((nx,) + share, jnp.bfloat16),
            pltpu.VMEM((hosts, 2) + share, jnp.bfloat16),
            pltpu.VMEM((hosts,) + share, jnp.bfloat16),
            pltpu.VMEM((hosts,) + share, jnp.bfloat16),
            pltpu.VMEM((2, block) + flat[1:], jnp.bfloat16),
            pltpu.VMEM((2, block) + flat[1:], jnp.bfloat16),
            pltpu.VMEM((doubled, doubled), jnp.float32),
            dma((nx,)), dma((nx,)), dma((hosts,)), dma((hosts,)), dma((hosts,)), dma((hosts,)),
            dma((2,)), dma((2,)),
        ],
        compiler_params=pltpu.CompilerParams(
            collective_id=0, has_side_effects=True, vmem_limit_bytes=VMEM_LIMIT
        ),
        name="reduce",
    )(partial.reshape((nx, ny) + share), field2, cot2)

    qb = 8
    z, spectral_grad = pl.pallas_call(
        modes_kernel,
        grid=(modes // qb,),
        out_shape=(
            jax.ShapeDtypeStruct(share, jnp.float32),
            jax.ShapeDtypeStruct((modes, count, channels, doubled), jnp.float32),
        ),
        in_specs=[
            pl.BlockSpec((count, qb, wide), lambda i: (0, i, 0)),
            pl.BlockSpec((qb, count, channels, doubled), lambda i: (i, 0, 0, 0)),
        ],
        out_specs=(
            pl.BlockSpec((count, qb, wide), lambda i: (0, i, 0)),
            pl.BlockSpec((qb, count, channels, doubled), lambda i: (i, 0, 0, 0)),
        ),
        compiler_params=params,
        name="modes",
    )(hat, spectral_weight)

    matrix = pltpu.VMEM((channels, channels), jnp.float32)
    everything, mix_grad = pl.pallas_call(
        functools.partial(
            gather_kernel, nx, 1.0 / math.sqrt(2 * total_x * total_y * pairs)
        ),
        out_shape=(
            jax.ShapeDtypeStruct((nx, ny) + share, jnp.bfloat16),
            jax.ShapeDtypeStruct((channels, channels), jnp.float32),
        ),
        in_specs=[vmem, vmem],
        out_specs=(vmem, vmem),
        scratch_shapes=[
            matrix, matrix, matrix, pltpu.VMEM((hosts, channels, channels), jnp.float32),
            dma((hosts,)), dma((hosts,)), dma((hosts,)), dma((hosts,)), dma((hosts,)),
            dma((nx,)), dma((nx,)), dma, dma, dma, dma, dma((hosts,)), dma((hosts,)),
        ],
        compiler_params=pltpu.CompilerParams(
            collective_id=1, has_side_effects=True, vmem_limit_bytes=VMEM_LIMIT
        ),
        name="gather",
    )(z, grad_part)

    empty = jnp.zeros_like(mix_weight)
    back = mix_weight.T
    rows = [
        [mix_weight if a == b else empty for b in range(2)] + [empty] * 2 for a in range(2)
    ] + [[empty] * 2 + [back if a == b else empty for b in range(2)] for a in range(2)]
    mixing = jnp.block(rows)
    mixed, field_grad = pl.pallas_call(
        functools.partial(inverse_kernel, modes),
        grid_spec=pltpu.PrefetchScalarGridSpec(
            num_scalar_prefetch=1,
            grid=grid,
            in_specs=[
                data_spec, data_spec, whole((groups, modes, wide)),
                one_of(ty_inv, 1), one_of(tx_inv, 0), whole(mixing.shape),
            ],
            out_specs=(data_spec, data_spec),
            scratch_shapes=[pltpu.VMEM((x_cells, SLOTS, pairs, wide), jnp.float32)],
        ),
        out_shape=(jax.ShapeDtypeStruct(flat, jnp.bfloat16),) * 2,
        compiler_params=params,
        name="inverse",
    )(where, field2, cot2, everything.reshape(groups, modes, wide), ty_inv, tx_inv, mixing)
    return (
        mixed.reshape(field.shape), field_grad.reshape(field.shape), spectral_grad, mix_grad
    )


def solution(mesh):
    placed = (
        P(("groups", "gx"), "gy", None, None),
        P(("groups", "gx"), "gy", None, None),
        P(None, ("gx", "gy"), None, None),
        P(),
    )
    return jax.shard_map(
        on_device,
        mesh=mesh,
        in_specs=placed,
        out_specs=(
            P(("groups", "gx"), "gy", None, None),
            P(("groups", "gx"), "gy", None, None),
            P("groups", ("gx", "gy"), None, None),
            P("groups", None),
        ),
        check_vma=False,
    )
```
